32 devices in a mesh: segment: 2 (over x), win: 4 (over z), mp: 4 (over y, core).
Axes of the slice: x: 2, y: 2, z: 4, core: 2. Of those that a mesh axis runs over, the one named last changes fastest.
Arguments:
- feats: bfloat16 [4, 1536, 256], P('win'), may hold values from -6 to 6
- convolution_kernel_weight: bfloat16 [1536, 5, 1536], P('win', None, 'mp'), may hold values from -0.0625 to 0.0625
- conv_bias: float32 [1536], P('mp'), may hold values from -3 to 3
- qkv_weight: bfloat16 [1536, 2560], P('win', 'mp'), may hold values from -0.15625 to 0.15625
- out_weight: bfloat16 [1536, 1536], P('win', 'mp'), may hold values from -0.15625 to 0.15625
- head_weight: bfloat16 [1536, 4096], P('win', 'mp'), may hold values from -0.15625 to 0.15625
- head_bias: float32 [4096], P('mp'), may hold values from -4 to 4
- exon_lists: int32 [3, 4, 8, 8], P(None, 'win'), may hold values from 0 to 256, as said below
Outputs:
- gene_tracks: float32 [64, 4096], P(('segment', 'win'), 'mp')
The draws below stay inside these ranges and needn't reach their ends.
Inputs may be any that keep to these rules, and one draw needn't show every extreme that they name: `exon_lists`: A slot with equal first and end bin is unused and has gene slot 0; used slots have 1 to 8 bins and a gene slot below 8. In every draw some owners receive 8 used ranges from every window.
All inputs are finite; a program needn't handle non-finite values.
Results may differ from the reference program's by a relative error of at most 0.0025.
Values may be sent and summed in bfloat16 or wider, within the bound.
No kernel may reach another device: no remote copies, remote signals or barrier semaphores. Data moves between devices by JAX's collectives and lax.ppermute only.
A program may use at most 64 MiB of HBM per device.

```python
import math
import jax
import jax.numpy as jnp
from jax import lax

D = 1536
HEADS = 8
KEY = 64
VAL = 192
TRACKS = 4096
KERNEL_TAPS = 5
DILATION_STEP = 4
WINDOW_BINS = 256
GENE_DEV = 8
CAP = 8
QKV = 2560
WINDOWS = 4
OWNERS = 8
GENES = 64


def draw_exon_lists(key, part):
    subkeys = jax.random.split(jax.random.fold_in(key, 17), 6)
    heavy_owner = jax.random.randint(subkeys[0], (OWNERS,), 0, 8) == 0
    forced_owner = jax.random.randint(subkeys[1], (), 0, OWNERS)
    heavy_owner = heavy_owner | (jnp.arange(OWNERS) == forced_owner)
    light_counts = jax.random.randint(subkeys[2], (WINDOWS, OWNERS), 0, CAP // 4 + 1)
    counts_all = jnp.where(heavy_owner[None, :], CAP, light_counts)
    is_live = jnp.arange(CAP)[None, None, :] < counts_all[:, :, None]
    range_cap = min(8, WINDOW_BINS)
    draw_shape = (WINDOWS, OWNERS, CAP)
    first_bins = jax.random.randint(subkeys[3], draw_shape, 0, WINDOW_BINS - range_cap + 1)
    lengths_drawn = jax.random.randint(subkeys[4], draw_shape, 1, range_cap + 1)
    gene_slots = jax.random.randint(subkeys[5], draw_shape, 0, GENE_DEV)
    starts = jnp.where(is_live, first_bins, 0)
    end_bins = jnp.where(is_live, first_bins + lengths_drawn, 0)
    gene_slots = jnp.where(is_live, gene_slots, 0)
    return jnp.stack([starts, end_bins, gene_slots]).astype(jnp.int32)


def block_levels(own_key, shape, cuts, least, high):
    loudness = 1.0
    for dim, blocks in cuts:
        draws = jax.random.uniform(jax.random.fold_in(jax.random.fold_in(own_key, 6), dim), (blocks,), jnp.float32, least / len(cuts), high / len(cuts))
        loudness = loudness * jnp.repeat(jnp.exp(draws), shape[dim] // blocks).reshape((-1,) + (1,) * (len(shape) - 1 - dim))
    return loudness


def centred(key, extent, deviation, most, shards=(), held_as=jnp.bfloat16):
    loudness = block_levels(key, extent, shards, -0.22, 0.18) if shards else 1.0
    drawn = jax.random.normal(key, extent, jnp.float32) * deviation * loudness
    return jnp.minimum(jnp.maximum(drawn, -most), most).astype(held_as)


def setup_inputs(seed: int = 0) -> dict:
    arg_keys = jax.random.split(jax.random.key(seed), 9)
    return {
        "feats": centred(arg_keys[0], (WINDOWS, D, WINDOW_BINS), 1.0, 6.0, ((0, 4),)),
        "convolution_kernel_weight": centred(arg_keys[1], (D, KERNEL_TAPS, D), (D * KERNEL_TAPS) ** -0.5, 0.0625, ((0, 4), (2, 4))),
        "conv_bias": centred(arg_keys[2], (D,), 0.5, 3.0, ((0, 4),), jnp.float32),
        "qkv_weight": centred(arg_keys[3], (D, QKV), D ** -0.5, 0.15625, ((0, 4), (1, 4))),
        "out_weight": centred(arg_keys[4], (D, HEADS * VAL), (HEADS * VAL) ** -0.5, 0.15625, ((0, 4), (1, 4))),
        "head_weight": centred(arg_keys[5], (D, TRACKS), D ** -0.5, 0.15625, ((0, 4), (1, 4))),
        "head_bias": centred(arg_keys[6], (TRACKS,), 1.0, 4.0, ((0, 4),), jnp.float32),
        "exon_lists": draw_exon_lists(jax.random.fold_in(arg_keys[8], 71), 0),
    }


def contract_rows(left, right):
    return lax.dot_general(left, right, (((0,), (0,)), ((), ())), preferred_element_type=jnp.float32)

def reference(feats, convolution_kernel_weight, conv_bias, qkv_weight, out_weight, head_weight, head_bias, exon_lists):
    receptive_reach_bins = (KERNEL_TAPS - 1) // 2 * DILATION_STEP
    head_span = 2 * KEY + VAL
    score_scale = 1.0 / math.sqrt(KEY)
    position = jnp.arange(WINDOW_BINS, dtype=jnp.int32)
    gene_ids = jnp.arange(GENES, dtype=jnp.int32)
    owner_base = (jnp.arange(OWNERS, dtype=jnp.int32) * GENE_DEV)[:, None]

    def one_window(gene_total, inputs):
        source, ranges = inputs
        padded_input = jnp.pad(source, ((0, 0), (receptive_reach_bins, receptive_reach_bins)))
        conv_pre = jnp.zeros((D, WINDOW_BINS), jnp.float32)
        for tap_index in range(KERNEL_TAPS):
            shifted_input = padded_input[:, tap_index * DILATION_STEP:tap_index * DILATION_STEP + WINDOW_BINS]
            conv_pre = conv_pre + contract_rows(convolution_kernel_weight[:, tap_index, :], shifted_input)
        conv_out = (source + jax.nn.gelu(conv_pre + conv_bias[:, None])).astype(jnp.bfloat16)
        qkv_rows = contract_rows(qkv_weight, conv_out).astype(jnp.bfloat16)
        outputs = []
        for head_idx in range(HEADS):
            offset = head_idx * head_span
            query_rows = qkv_rows[offset:offset + KEY]
            key_rows = qkv_rows[offset + KEY:offset + 2 * KEY]
            value_rows = qkv_rows[offset + 2 * KEY:offset + head_span]
            scores = contract_rows(query_rows, key_rows) * score_scale
            weights = jnp.exp(scores)
            prob_rows = (weights / lax.optimization_barrier(jnp.sum(weights, axis=1, keepdims=True))).astype(jnp.bfloat16)
            head_out = lax.dot_general(value_rows, prob_rows, (((1,), (1,)), ((), ())), preferred_element_type=jnp.float32)
            outputs.append(head_out.astype(jnp.bfloat16))
        joined = jnp.concatenate(outputs, axis=0)
        attn_out = lax.dot_general(out_weight, joined, (((1,), (0,)), ((), ())), preferred_element_type=jnp.float32)
        resid = (conv_out + attn_out).astype(jnp.bfloat16)
        logits = contract_rows(head_weight, resid) + head_bias[:, None]
        tracks = jax.nn.softplus(logits).astype(jnp.bfloat16)
        starts = ranges[0].reshape(-1)
        end_bins = ranges[1].reshape(-1)
        inside = (position[None, :] >= starts[:, None]) & (position[None, :] < end_bins[:, None])
        entry_sum = lax.dot_general(inside.astype(jnp.bfloat16), tracks, (((1,), (1,)), ((), ())), preferred_element_type=jnp.float32)
        global_ids = (ranges[2] + owner_base).reshape(-1)
        onehot = (global_ids[:, None] == gene_ids[None, :]).astype(jnp.float32)
        gene_total = gene_total + lax.dot_general(onehot, entry_sum, (((0,), (0,)), ((), ())), precision=lax.Precision.HIGHEST, preferred_element_type=jnp.float32)
        return (gene_total, None)
    ranges_all = jnp.moveaxis(exon_lists, 1, 0)
    gene_total, unused = lax.scan(one_window, jnp.zeros((GENES, TRACKS), jnp.float32), (feats, ranges_all))
    return jnp.log1p(gene_total)
```

```python
import functools
import math

import jax
import jax.numpy as jnp
from jax import lax
from jax.experimental import pallas as pl
from jax.experimental.pallas import tpu as pltpu
from jax.sharding import PartitionSpec as P

KEY = 64
VAL = 192
DILATION_STEP = 4
GENE_DEV = 8
SPAN = 2 * KEY + VAL
VMEM_BYTES = 40 * 1024 * 1024
F32 = jnp.float32
BF16 = jnp.bfloat16


def call_kernel(body, out_shape, *operands, flops=0):
    whole = pl.BlockSpec(memory_space=pltpu.VMEM)
    return pl.pallas_call(
        body,
        out_shape=out_shape,
        in_specs=[whole] * len(operands),
        out_specs=whole,
        compiler_params=pltpu.CompilerParams(vmem_limit_bytes=VMEM_BYTES),
        cost_estimate=pl.CostEstimate(flops=flops, bytes_accessed=1 << 20, transcendentals=0),
    )(*operands)


def shifted(x, axis, by):
    size = lax.axis_size(axis)
    return lax.ppermute(x, axis, [(i, (i + by) % size) for i in range(size)])


def conv_kernel(x_ref, w_ref, o_ref):
    bins = o_ref.shape[0]
    x = x_ref[...].astype(F32)
    total = jnp.zeros(o_ref.shape, F32)
    for tap in range(w_ref.shape[0]):
        start = tap * DILATION_STEP
        total += jnp.dot(
            x[start : start + bins].astype(BF16), w_ref[tap], preferred_element_type=F32
        )
    o_ref[...] = total.astype(o_ref.dtype)


def joined_bins(blocks_ref, segments):
    models = blocks_ref.shape[0] // segments
    rows = [
        jnp.concatenate([blocks_ref[s * models + m] for m in range(models)], axis=1)
        for s in range(segments)
    ]
    return jnp.concatenate(rows, axis=0)


def attention_kernel(segments, x_ref, qkv_ref, out_ref, o_ref):
    x = joined_bins(x_ref, segments)
    models = o_ref.shape[0] // segments
    bins, cols = o_ref.shape[1:]
    total = None
    for head in range(qkv_ref.shape[1] // SPAN):
        rows = jnp.dot(
            x, qkv_ref[:, head * SPAN : (head + 1) * SPAN], preferred_element_type=F32
        ).astype(BF16)
        query, key, value = rows[:, :KEY], rows[:, KEY : 2 * KEY], rows[:, 2 * KEY :]
        scores = lax.dot_general(
            query, key, (((1,), (1,)), ((), ())), preferred_element_type=F32
        ) * (1.0 / math.sqrt(KEY))
        weights = jnp.exp(scores)
        probs = (weights / jnp.sum(weights, axis=1, keepdims=True)).astype(BF16)
        att = jnp.dot(probs, value, preferred_element_type=F32).astype(BF16)
        term = lax.dot_general(
            att,
            out_ref[:, head * VAL : (head + 1) * VAL],
            (((1,), (1,)), ((), ())),
            preferred_element_type=F32,
        )
        total = term if total is None else total + term
    total = total.astype(o_ref.dtype)
    for s in range(segments):
        for m in range(models):
            o_ref[s * models + m] = total[s * bins : (s + 1) * bins, m * cols : (m + 1) * cols]


def head_kernel(segments, x_ref, w_ref, b_ref, counts_ref, o_ref):
    x = joined_bins(x_ref, segments)
    logits = jnp.dot(x, w_ref[...], preferred_element_type=F32) + b_ref[...]
    tracks = jax.nn.softplus(logits).astype(BF16)
    sums = jnp.dot(counts_ref[...], tracks, preferred_element_type=F32)
    o_ref[...] = sums.astype(o_ref.dtype)


def gene_counts(ranges, bins):
    position = jnp.arange(bins, dtype=jnp.int32)
    inside = (position >= ranges[0][:, :, None]) & (position < ranges[1][:, :, None])
    slots = jnp.arange(GENE_DEV, dtype=jnp.int32)
    chosen = ranges[2][:, None, :] == slots[None, :, None]
    counts = jnp.sum(
        (chosen[..., None] & inside[:, None]).astype(F32), axis=2
    )
    return counts.reshape(-1, bins).astype(BF16)


def local(
    feats,
    convolution_kernel_weight,
    conv_bias,
    qkv_weight,
    out_weight,
    head_weight,
    head_bias,
    exon_lists,
):
    segment_index = lax.axis_index("segment")
    win_index = lax.axis_index("win")
    model_index = lax.axis_index("mp")
    segments, windows, models = (lax.axis_size(a) for a in ("segment", "win", "mp"))
    chan_count, bin_count = feats.shape[1:]
    row_count, tap_count, out_cols = convolution_kernel_weight.shape
    bins = bin_count // segments
    reach = (tap_count - 1) // 2 * DILATION_STEP
    plane = ("segment", "mp")

    def part_of_segment(x):
        size = x.shape[1] // segments
        return lax.dynamic_slice_in_dim(x, segment_index * size, size, 1)

    qkv_full = lax.all_gather(part_of_segment(qkv_weight), "win", axis=0, tiled=True)
    out_full = lax.all_gather(part_of_segment(out_weight), "win", axis=0, tiled=True)
    head_full = lax.all_gather(part_of_segment(head_weight), "win", axis=0, tiled=True)
    track_cols = head_full.shape[1]
    bias_part = lax.dynamic_slice_in_dim(head_bias, segment_index * track_cols, track_cols, 0)
    counts = gene_counts(exon_lists[:, 0], bin_count)

    taps = jnp.transpose(convolution_kernel_weight, (1, 0, 2))
    padded = jnp.pad(feats[0].T, ((reach, reach), (0, 0)))
    own_bins = lax.dynamic_slice_in_dim(padded, segment_index * bins, bins + 2 * reach, 0)

    def rows_for(window):
        return lax.dynamic_slice_in_dim(own_bins, window * row_count, row_count, 1)

    def conv_of(x, dtype):
        return call_kernel(
            conv_kernel,
            jax.ShapeDtypeStruct((bins, out_cols), dtype),
            x,
            taps,
            flops=2 * bins * out_cols * row_count * tap_count,
        )

    if windows <= 8:
        arrived = [
            shifted(rows_for(lax.rem(win_index + by, windows)), "win", by)
            for by in range(1, windows)
        ]
        conv_pre = conv_of(rows_for(win_index), F32)
        for by, x in enumerate(arrived, 1):
            conv_pre = conv_pre + shifted(conv_of(x, BF16), "win", -by).astype(F32)
    else:
        blocks = own_bins.reshape(own_bins.shape[0], windows, row_count).transpose(1, 0, 2)
        arrived = lax.all_to_all(blocks, "win", 0, 0, tiled=True)
        partial = jnp.stack([conv_of(arrived[w], BF16) for w in range(windows)])
        conv_pre = lax.all_to_all(partial, "win", 0, 0, tiled=True).astype(F32).sum(axis=0)

    own_feats = lax.dynamic_slice(own_bins, (reach, model_index * out_cols), (bins, out_cols))
    conv_out = (own_feats + jax.nn.gelu(conv_pre + conv_bias)).astype(BF16)
    all_chan = lax.all_gather(conv_out, plane, axis=0)

    partial = call_kernel(
        functools.partial(attention_kernel, segments),
        jax.ShapeDtypeStruct(all_chan.shape, BF16),
        all_chan,
        qkv_full,
        out_full,
    )
    summed = lax.all_to_all(partial, plane, 0, 0, tiled=True).astype(F32).sum(axis=0)
    resid = (conv_out.astype(F32) + summed).astype(BF16)
    all_resid = lax.all_gather(resid, plane, axis=0)

    sums = call_kernel(
        functools.partial(head_kernel, segments),
        jax.ShapeDtypeStruct((counts.shape[0], track_cols), BF16),
        all_resid,
        head_full,
        bias_part[None, :],
        counts,
    )
    owners = segments * windows
    got = lax.all_to_all(
        sums.reshape(owners, GENE_DEV, track_cols), ("segment", "win"), 0, 0, tiled=True
    )
    got = got.astype(F32).reshape(segments, windows, GENE_DEV, track_cols).sum(axis=1)
    return jnp.log1p(got.transpose(1, 0, 2).reshape(GENE_DEV, segments * track_cols))


def solution(mesh):
    in_specs = (
        P("win", None, None),
        P("win", None, "mp"),
        P("mp"),
        P("win", "mp"),
        P("win", "mp"),
        P("win", "mp"),
        P("mp"),
        P(None, "win", None, None),
    )
    out_specs = P(("segment", "win"), "mp")
    return jax.shard_map(local, mesh=mesh, in_specs=in_specs, out_specs=out_specs, check_vma=False)
```

```python
import functools
import math

import jax
import jax.numpy as jnp
from jax import lax
from jax.experimental import pallas as pl
from jax.experimental.pallas import tpu as pltpu
from jax.sharding import PartitionSpec as P

KEY = 64
VAL = 192
DILATION_STEP = 4
GENE_DEV = 8
SPAN = 2 * KEY + VAL
VMEM_BYTES = 40 * 1024 * 1024
F32 = jnp.float32
BF16 = jnp.bfloat16


def call_kernel(body, out_shape, *operands, flops=0):
    whole = pl.BlockSpec(memory_space=pltpu.VMEM)
    scalars = pl.BlockSpec(memory_space=pltpu.SMEM)
    return pl.pallas_call(
        body,
        out_shape=out_shape,
        in_specs=[scalars if x.dtype == jnp.int32 else whole for x in operands],
        out_specs=whole,
        compiler_params=pltpu.CompilerParams(vmem_limit_bytes=VMEM_BYTES),
        cost_estimate=pl.CostEstimate(flops=flops, bytes_accessed=1 << 20, transcendentals=0),
    )(*operands)


def shifted(x, axis, by):
    size = lax.axis_size(axis)
    return lax.ppermute(x, axis, [(i, (i + by) % size) for i in range(size)])


def conv_kernel(x_ref, w_ref, o_ref):
    bins = o_ref.shape[0]
    x = x_ref[...].astype(F32)
    total = jnp.zeros(o_ref.shape, F32)
    for tap in range(w_ref.shape[0]):
        start = tap * DILATION_STEP
        total += jnp.dot(
            x[start : start + bins].astype(BF16), w_ref[tap], preferred_element_type=F32
        )
    o_ref[...] = total.astype(o_ref.dtype)


def block_of(win_ref, by, windows):
    return lax.rem(win_ref[0] + windows - by, windows)


def contract_blocks(x_ref, segments, win_ref, pieces, cols):
    models = x_ref.shape[0] // segments
    total = None
    for by, piece in enumerate(pieces):
        if len(pieces) == 1:
            rows = [
                jnp.concatenate([x_ref[s * models + m] for m in range(models)], axis=1)
                for s in range(segments)
            ]
        else:
            block = block_of(win_ref, by, len(pieces))
            rows = [x_ref[s * models + block] for s in range(segments)]
        term = jnp.dot(jnp.concatenate(rows, axis=0), piece[:, cols], preferred_element_type=F32)
        total = term if total is None else total + term
    return total


def attention_kernel(segments, heads, win_ref, x_ref, *refs):
    *pieces, o_ref = refs
    models = o_ref.shape[0] // segments
    bins = o_ref.shape[1]
    width = o_ref.shape[2]
    rows = contract_blocks(x_ref, segments, win_ref, pieces, slice(0, heads * SPAN)).astype(BF16)
    outputs = []
    for head in range(heads):
        own = rows[:, head * SPAN : (head + 1) * SPAN]
        query, key, value = own[:, :KEY], own[:, KEY : 2 * KEY], own[:, 2 * KEY :]
        scores = lax.dot_general(
            query, key, (((1,), (1,)), ((), ())), preferred_element_type=F32
        ) * (1.0 / math.sqrt(KEY))
        weights = jnp.exp(scores)
        probs = (weights / jnp.sum(weights, axis=1, keepdims=True)).astype(BF16)
        outputs.append(jnp.dot(probs, value, preferred_element_type=F32).astype(BF16))
    att = jnp.concatenate(outputs, axis=1)
    for by, piece in enumerate(pieces):
        term = lax.dot_general(
            att,
            piece[:, heads * SPAN :],
            (((1,), (1,)), ((), ())),
            preferred_element_type=F32,
        ).astype(o_ref.dtype)
        for s in range(segments):
            own = term[s * bins : (s + 1) * bins]
            if len(pieces) > 1:
                o_ref[s * models + block_of(win_ref, by, len(pieces))] = own
            else:
                for m in range(models):
                    o_ref[s * models + m] = own[:, m * width : (m + 1) * width]


def head_kernel(segments, win_ref, x_ref, b_ref, counts_ref, *refs):
    *pieces, o_ref = refs
    logits = contract_blocks(x_ref, segments, win_ref, pieces, slice(None)) + b_ref[...]
    tracks = jax.nn.softplus(logits).astype(BF16)
    sums = jnp.dot(counts_ref[...], tracks, preferred_element_type=F32)
    o_ref[...] = sums.astype(o_ref.dtype)


def gene_counts(ranges, bins):
    position = jnp.arange(bins, dtype=jnp.int32)
    inside = (position >= ranges[0][:, :, None]) & (position < ranges[1][:, :, None])
    slots = jnp.arange(GENE_DEV, dtype=jnp.int32)
    chosen = ranges[2][:, None, :] == slots[None, :, None]
    counts = jnp.sum(
        (chosen[..., None] & inside[:, None]).astype(F32), axis=2
    )
    return counts.reshape(-1, bins).astype(BF16)


def local(
    feats,
    convolution_kernel_weight,
    conv_bias,
    qkv_weight,
    out_weight,
    head_weight,
    head_bias,
    exon_lists,
):
    segment_index = lax.axis_index("segment")
    win_index = lax.axis_index("win")
    model_index = lax.axis_index("mp")
    segments, windows, models = (lax.axis_size(a) for a in ("segment", "win", "mp"))
    chan_count, bin_count = feats.shape[1:]
    row_count, tap_count, out_cols = convolution_kernel_weight.shape
    bins = bin_count // segments
    reach = (tap_count - 1) // 2 * DILATION_STEP
    plane = ("segment", "mp")

    def part_of_segment(x):
        size = x.shape[1] // segments
        return lax.dynamic_slice_in_dim(x, segment_index * size, size, 1)

    attention_own = jnp.concatenate(
        [part_of_segment(qkv_weight), part_of_segment(out_weight)], axis=1
    )
    head_own = part_of_segment(head_weight)
    heads = qkv_weight.shape[1] // segments // SPAN
    stepwise = windows <= 8 and row_count == out_cols

    def gathered(own, after):
        if not stepwise:
            return [lax.all_gather(own, "win", axis=0, tiled=True)]
        sent, _ = lax.optimization_barrier((own, after))
        return [own] + [shifted(sent, "win", by) for by in range(1, windows)]

    win_ref = win_index.astype(jnp.int32)[None]
    track_cols = head_own.shape[1]
    bias_part = lax.dynamic_slice_in_dim(head_bias, segment_index * track_cols, track_cols, 0)
    counts = gene_counts(exon_lists[:, 0], bin_count)

    taps = jnp.transpose(convolution_kernel_weight, (1, 0, 2))
    padded = jnp.pad(feats[0].T, ((reach, reach), (0, 0)))
    own_bins = lax.dynamic_slice_in_dim(padded, segment_index * bins, bins + 2 * reach, 0)

    def rows_for(window):
        return lax.dynamic_slice_in_dim(own_bins, window * row_count, row_count, 1)

    def conv_of(x, dtype):
        return call_kernel(
            conv_kernel,
            jax.ShapeDtypeStruct((bins, out_cols), dtype),
            x,
            taps,
            flops=2 * bins * out_cols * row_count * tap_count,
        )

    if stepwise:
        arrived = [
            shifted(rows_for(lax.rem(win_index + by, windows)), "win", by)
            for by in range(1, windows)
        ]
        attention_pieces = gathered(attention_own, arrived)
        conv_pre = conv_of(rows_for(win_index), F32)
        for by, x in enumerate(arrived, 1):
            conv_pre = conv_pre + shifted(conv_of(x, BF16), "win", -by).astype(F32)
    else:
        blocks = own_bins.reshape(own_bins.shape[0], windows, row_count).transpose(1, 0, 2)
        arrived = lax.all_to_all(blocks, "win", 0, 0, tiled=True)
        attention_pieces = gathered(attention_own, None)
        partial = jnp.stack([conv_of(arrived[w], BF16) for w in range(windows)])
        conv_pre = lax.all_to_all(partial, "win", 0, 0, tiled=True).astype(F32).sum(axis=0)

    own_feats = lax.dynamic_slice(own_bins, (reach, model_index * out_cols), (bins, out_cols))
    conv_out = (own_feats + jax.nn.gelu(conv_pre + conv_bias)).astype(BF16)
    head_pieces = gathered(head_own, conv_out)
    all_chan = lax.all_gather(conv_out, plane, axis=0)

    partial = call_kernel(
        functools.partial(attention_kernel, segments, heads),
        jax.ShapeDtypeStruct(all_chan.shape, BF16),
        win_ref,
        all_chan,
        *attention_pieces,
    )
    summed = lax.all_to_all(partial, plane, 0, 0, tiled=True).astype(F32).sum(axis=0)
    resid = (conv_out.astype(F32) + summed).astype(BF16)
    all_resid = lax.all_gather(resid, plane, axis=0)

    sums = call_kernel(
        functools.partial(head_kernel, segments),
        jax.ShapeDtypeStruct((counts.shape[0], track_cols), BF16),
        win_ref,
        all_resid,
        bias_part[None, :],
        counts,
        *head_pieces,
    )
    owners = segments * windows
    got = lax.all_to_all(
        sums.reshape(owners, GENE_DEV, track_cols), ("segment", "win"), 0, 0, tiled=True
    )
    got = got.astype(F32).reshape(segments, windows, GENE_DEV, track_cols).sum(axis=1)
    return jnp.log1p(got.transpose(1, 0, 2).reshape(GENE_DEV, segments * track_cols))


def solution(mesh):
    in_specs = (
        P("win", None, None),
        P("win", None, "mp"),
        P("mp"),
        P("win", "mp"),
        P("win", "mp"),
        P("win", "mp"),
        P("mp"),
        P(None, "win", None, None),
    )
    out_specs = P(("segment", "win"), "mp")
    return jax.shard_map(local, mesh=mesh, in_specs=in_specs, out_specs=out_specs, check_vma=False)
```

```python
import functools
import math

import jax
import jax.numpy as jnp
from jax import lax
from jax.experimental import pallas as pl
from jax.experimental.pallas import tpu as pltpu
from jax.sharding import PartitionSpec as P

KEY = 64
VAL = 192
DILATION_STEP = 4
GENE_DEV = 8
SPAN = 2 * KEY + VAL
VMEM_BYTES = 40 * 1024 * 1024
F32 = jnp.float32
BF16 = jnp.bfloat16


def call_kernel(body, out_shape, *operands, flops=0):
    whole = pl.BlockSpec(memory_space=pltpu.VMEM)
    scalars = pl.BlockSpec(memory_space=pltpu.SMEM)
    return pl.pallas_call(
        body,
        out_shape=out_shape,
        in_specs=[scalars if x.dtype == jnp.int32 else whole for x in operands],
        out_specs=whole,
        compiler_params=pltpu.CompilerParams(vmem_limit_bytes=VMEM_BYTES),
        cost_estimate=pl.CostEstimate(flops=flops, bytes_accessed=1 << 20, transcendentals=0),
    )(*operands)


def shifted(x, axis, by):
    size = lax.axis_size(axis)
    return lax.ppermute(x, axis, [(i, (i + by) % size) for i in range(size)])


def conv_kernel(x_ref, w_ref, o_ref):
    bins = o_ref.shape[0]
    x = x_ref[...].astype(F32)
    total = jnp.zeros(o_ref.shape, F32)
    for tap in range(w_ref.shape[0]):
        start = tap * DILATION_STEP
        total += jnp.dot(
            x[start : start + bins].astype(BF16), w_ref[tap], preferred_element_type=F32
        )
    o_ref[...] = total.astype(o_ref.dtype)


def block_of(win_ref, by, windows):
    return lax.rem(win_ref[0] + windows - by, windows)


def contract_blocks(x_ref, segments, win_ref, pieces, cols):
    models = x_ref.shape[0] // segments
    total = None
    for by, piece in enumerate(pieces):
        if len(pieces) == 1:
            rows = [
                jnp.concatenate([x_ref[s * models + m] for m in range(models)], axis=1)
                for s in range(segments)
            ]
        else:
            block = block_of(win_ref, by, len(pieces))
            rows = [x_ref[s * models + block] for s in range(segments)]
        term = jnp.dot(jnp.concatenate(rows, axis=0), piece[:, cols], preferred_element_type=F32)
        total = term if total is None else total + term
    return total


def attention_kernel(segments, heads, win_ref, x_ref, *refs):
    *pieces, o_ref = refs
    models = o_ref.shape[0] // segments
    bins = o_ref.shape[1]
    width = o_ref.shape[2]
    rows = contract_blocks(x_ref, segments, win_ref, pieces, slice(0, heads * SPAN)).astype(BF16)
    outputs = []
    for head in range(heads):
        own = rows[:, head * SPAN : (head + 1) * SPAN]
        query, key, value = own[:, :KEY], own[:, KEY : 2 * KEY], own[:, 2 * KEY :]
        scores = lax.dot_general(
            query, key, (((1,), (1,)), ((), ())), preferred_element_type=F32
        ) * (1.0 / math.sqrt(KEY))
        weights = jnp.exp(scores)
        probs = (weights / jnp.sum(weights, axis=1, keepdims=True)).astype(BF16)
        outputs.append(jnp.dot(probs, value, preferred_element_type=F32).astype(BF16))
    att = jnp.concatenate(outputs, axis=1)
    for by, piece in enumerate(pieces):
        term = lax.dot_general(
            att,
            piece[:, heads * SPAN :],
            (((1,), (1,)), ((), ())),
            preferred_element_type=F32,
        ).astype(o_ref.dtype)
        for s in range(segments):
            own = term[s * bins : (s + 1) * bins]
            if len(pieces) > 1:
                o_ref[s * models + block_of(win_ref, by, len(pieces))] = own
            else:
                for m in range(models):
                    o_ref[s * models + m] = own[:, m * width : (m + 1) * width]


def head_kernel(segments, win_ref, x_ref, b_ref, counts_ref, *refs):
    *pieces, o_ref = refs
    logits = contract_blocks(x_ref, segments, win_ref, pieces, slice(None)) + b_ref[...]
    tracks = jax.nn.softplus(logits).astype(BF16)
    sums = jnp.dot(counts_ref[...], tracks, preferred_element_type=F32)
    o_ref[...] = sums.astype(o_ref.dtype)


def gene_counts(ranges, bins):
    position = jnp.arange(bins, dtype=jnp.int32)
    inside = (position >= ranges[0][:, :, None]) & (position < ranges[1][:, :, None])
    slots = jnp.arange(GENE_DEV, dtype=jnp.int32)
    chosen = ranges[2][:, None, :] == slots[None, :, None]
    counts = jnp.sum(
        (chosen[..., None] & inside[:, None]).astype(F32), axis=2
    )
    return counts.reshape(-1, bins).astype(BF16)


def local(
    feats,
    convolution_kernel_weight,
    conv_bias,
    qkv_weight,
    out_weight,
    head_weight,
    head_bias,
    exon_lists,
):
    segment_index = lax.axis_index("segment")
    win_index = lax.axis_index("win")
    model_index = lax.axis_index("mp")
    segments, windows, models = (lax.axis_size(a) for a in ("segment", "win", "mp"))
    chan_count, bin_count = feats.shape[1:]
    row_count, tap_count, out_cols = convolution_kernel_weight.shape
    bins = bin_count // segments
    reach = (tap_count - 1) // 2 * DILATION_STEP
    plane = ("segment", "mp")

    def part_of_segment(x):
        size = x.shape[1] // segments
        return lax.dynamic_slice_in_dim(x, segment_index * size, size, 1)

    attention_own = jnp.concatenate(
        [part_of_segment(qkv_weight), part_of_segment(out_weight)], axis=1
    )
    head_own = part_of_segment(head_weight)
    heads = qkv_weight.shape[1] // segments // SPAN
    stepwise = windows <= 8 and row_count == out_cols

    def gathered(own, after):
        if not stepwise:
            return [lax.all_gather(own, "win", axis=0, tiled=True)]
        sent, _ = lax.optimization_barrier((own, after))
        if windows != 4:
            return [own] + [shifted(sent, "win", by) for by in range(1, windows)]
        below, above = shifted(sent, "win", 1), shifted(sent, "win", -1)
        handed = jnp.where(win_index == 1, above, jnp.where(win_index == 2, below, sent))
        across = lax.ppermute(handed, "win", [(0, 2), (1, 0), (2, 3), (3, 1)])
        return [own, below, across, above]

    win_ref = win_index.astype(jnp.int32)[None]
    track_cols = head_own.shape[1]
    bias_part = lax.dynamic_slice_in_dim(head_bias, segment_index * track_cols, track_cols, 0)
    counts = gene_counts(exon_lists[:, 0], bin_count)

    taps = jnp.transpose(convolution_kernel_weight, (1, 0, 2))
    padded = jnp.pad(feats[0].T, ((reach, reach), (0, 0)))
    own_bins = lax.dynamic_slice_in_dim(padded, segment_index * bins, bins + 2 * reach, 0)

    def rows_for(window):
        return lax.dynamic_slice_in_dim(own_bins, window * row_count, row_count, 1)

    def conv_of(x, dtype):
        return call_kernel(
            conv_kernel,
            jax.ShapeDtypeStruct((bins, out_cols), dtype),
            x,
            taps,
            flops=2 * bins * out_cols * row_count * tap_count,
        )

    if stepwise:
        arrived = [
            shifted(rows_for(lax.rem(win_index + by, windows)), "win", by)
            for by in range(1, windows)
        ]
        attention_pieces = gathered(attention_own, arrived)
        conv_pre = conv_of(rows_for(win_index), F32)
        for by, x in enumerate(arrived, 1):
            conv_pre = conv_pre + shifted(conv_of(x, BF16), "win", -by).astype(F32)
    else:
        blocks = own_bins.reshape(own_bins.shape[0], windows, row_count).transpose(1, 0, 2)
        arrived = lax.all_to_all(blocks, "win", 0, 0, tiled=True)
        attention_pieces = gathered(attention_own, None)
        partial = jnp.stack([conv_of(arrived[w], BF16) for w in range(windows)])
        conv_pre = lax.all_to_all(partial, "win", 0, 0, tiled=True).astype(F32).sum(axis=0)

    own_feats = lax.dynamic_slice(own_bins, (reach, model_index * out_cols), (bins, out_cols))
    conv_out = (own_feats + jax.nn.gelu(conv_pre + conv_bias)).astype(BF16)
    head_pieces = gathered(head_own, conv_out)
    all_chan = lax.all_gather(conv_out, plane, axis=0)

    partial = call_kernel(
        functools.partial(attention_kernel, segments, heads),
        jax.ShapeDtypeStruct(all_chan.shape, BF16),
        win_ref,
        all_chan,
        *attention_pieces,
    )
    summed = lax.all_to_all(partial, plane, 0, 0, tiled=True).astype(F32).sum(axis=0)
    resid = (conv_out.astype(F32) + summed).astype(BF16)
    all_resid = lax.all_gather(resid, plane, axis=0)

    sums = call_kernel(
        functools.partial(head_kernel, segments),
        jax.ShapeDtypeStruct((counts.shape[0], track_cols), BF16),
        win_ref,
        all_resid,
        bias_part[None, :],
        counts,
        *head_pieces,
    )
    owners = segments * windows
    got = lax.all_to_all(
        sums.reshape(owners, GENE_DEV, track_cols), ("segment", "win"), 0, 0, tiled=True
    )
    got = got.astype(F32).reshape(segments, windows, GENE_DEV, track_cols).sum(axis=1)
    return jnp.log1p(got.transpose(1, 0, 2).reshape(GENE_DEV, segments * track_cols))


def solution(mesh):
    in_specs = (
        P("win", None, None),
        P("win", None, "mp"),
        P("mp"),
        P("win", "mp"),
        P("win", "mp"),
        P("win", "mp"),
        P("mp"),
        P(None, "win", None, None),
    )
    out_specs = P(("segment", "win"), "mp")
    return jax.shard_map(local, mesh=mesh, in_specs=in_specs, out_specs=out_specs, check_vma=False)
```

```python
import functools
import math

import jax
import jax.numpy as jnp
from jax import lax
from jax.experimental import pallas as pl
from jax.experimental.pallas import tpu as pltpu
from jax.sharding import PartitionSpec as P

KEY = 64
VAL = 192
DILATION_STEP = 4
GENE_DEV = 8
SPAN = 2 * KEY + VAL
VMEM_BYTES = 40 * 1024 * 1024
F32 = jnp.float32
BF16 = jnp.bfloat16


def call_kernel(body, out_shape, *operands, scratch=(), flops=0):
    whole = pl.BlockSpec(memory_space=pltpu.VMEM)
    scalars = pl.BlockSpec(memory_space=pltpu.SMEM)
    return pl.pallas_call(
        body,
        out_shape=out_shape,
        in_specs=[scalars if x.dtype == jnp.int32 else whole for x in operands],
        out_specs=jax.tree.map(lambda _: whole, out_shape),
        scratch_shapes=list(scratch),
        compiler_params=pltpu.CompilerParams(vmem_limit_bytes=VMEM_BYTES),
        cost_estimate=pl.CostEstimate(flops=flops, bytes_accessed=1 << 20, transcendentals=0),
    )(*operands)


def shifted(x, axis, by):
    size = lax.axis_size(axis)
    return lax.ppermute(x, axis, [(i, (i + by) % size) for i in range(size)])


def bins_kernel(place_ref, x_ref, own_ref, next_ref, part_ref, rest_ref, padded):
    segment, window, model = place_ref[0], place_ref[1], place_ref[2]
    odd = lax.rem(model, 2)
    bins = rest_ref.shape[0]
    margin = (own_ref.shape[0] - bins) // 2
    start = segment * bins
    padded[:margin] = jnp.zeros((margin, padded.shape[1]), F32)
    padded[padded.shape[0] - margin :] = jnp.zeros((margin, padded.shape[1]), F32)

    def turned(block):
        first = pl.multiple_of(block * padded.shape[1], 16)
        columns = x_ref[pl.ds(first, padded.shape[1]), :].astype(F32)
        padded[margin : padded.shape[0] - margin] = columns.T

    def cut(out, first):
        out[...] = padded[pl.ds(pl.multiple_of(start + first, 8), out.shape[0])].astype(BF16)

    turned(lax.rem(window + 1 + 2 * odd, 4))
    cut(next_ref, 0)
    turned(lax.rem(window + 2, 4))
    cut(part_ref, odd * (own_ref.shape[0] - part_ref.shape[0]))
    turned(window)
    cut(own_ref, 0)
    turned(model)
    cut(rest_ref, margin)


def pack_kernel(place_ref, *refs):
    *parts, o_ref = refs
    segments = sum(x.shape[1] for x in parts) // o_ref.shape[1]
    for s in range(segments):

        @pl.when(place_ref[0] == s)
        def _():
            at = 0
            for x in parts:
                width = x.shape[1] // segments
                o_ref[:, at : at + width] = x[:, s * width : (s + 1) * width]
                at += width


def conv_kernel(x_ref, w_ref, o_ref):
    taps(x_ref[...].astype(F32), w_ref, o_ref)


def parts_conv_kernel(place_ref, own_ref, other_ref, w_ref, o_ref):
    even = lax.rem(place_ref[2], 2) == 0
    own, other = own_ref[...].astype(F32), other_ref[...].astype(F32)
    rows = o_ref.shape[0] + (w_ref.shape[0] - 1) * DILATION_STEP
    low = jnp.where(even, own, other)
    high = jnp.where(even, other, own)[2 * own.shape[0] - rows :]
    taps(jnp.concatenate([low, high], axis=0), w_ref, o_ref)


def taps(x, w_ref, o_ref):
    bins = o_ref.shape[0]
    total = jnp.zeros(o_ref.shape, F32)
    for tap in range(w_ref.shape[0]):
        start = tap * DILATION_STEP
        total += jnp.dot(
            x[start : start + bins].astype(BF16), w_ref[tap], preferred_element_type=F32
        )
    o_ref[...] = total.astype(o_ref.dtype)


def block_of(win_ref, by, windows):
    return lax.rem(win_ref[0] + windows - by, windows)


def contract_blocks(x_ref, segments, win_ref, pieces, cols):
    models = x_ref.shape[0] // segments
    total = None
    for by, piece in enumerate(pieces):
        if len(pieces) == 1:
            rows = [
                jnp.concatenate([x_ref[s * models + m] for m in range(models)], axis=1)
                for s in range(segments)
            ]
        else:
            block = block_of(win_ref, by, len(pieces))
            rows = [x_ref[s * models + block] for s in range(segments)]
        term = jnp.dot(jnp.concatenate(rows, axis=0), piece[:, cols], preferred_element_type=F32)
        total = term if total is None else total + term
    return total


def attention_kernel(segments, heads, win_ref, x_ref, *refs):
    *pieces, o_ref = refs
    models = o_ref.shape[0] // segments
    bins = o_ref.shape[1]
    width = o_ref.shape[2]
    rows = contract_blocks(x_ref, segments, win_ref, pieces, slice(0, heads * SPAN)).astype(BF16)
    outputs = []
    for head in range(heads):
        own = rows[:, head * SPAN : (head + 1) * SPAN]
        query, key, value = own[:, :KEY], own[:, KEY : 2 * KEY], own[:, 2 * KEY :]
        scores = lax.dot_general(
            query, key, (((1,), (1,)), ((), ())), preferred_element_type=F32
        ) * (1.0 / math.sqrt(KEY))
        weights = jnp.exp(scores)
        probs = (weights / jnp.sum(weights, axis=1, keepdims=True)).astype(BF16)
        outputs.append(jnp.dot(probs, value, preferred_element_type=F32).astype(BF16))
    att = jnp.concatenate(outputs, axis=1)
    for by, piece in enumerate(pieces):
        term = lax.dot_general(
            att,
            piece[:, heads * SPAN :],
            (((1,), (1,)), ((), ())),
            preferred_element_type=F32,
        ).astype(o_ref.dtype)
        for s in range(segments):
            own = term[s * bins : (s + 1) * bins]
            if len(pieces) > 1:
                o_ref[s * models + block_of(win_ref, by, len(pieces))] = own
            else:
                for m in range(models):
                    o_ref[s * models + m] = own[:, m * width : (m + 1) * width]


def head_kernel(segments, win_ref, x_ref, b_ref, counts_ref, *refs):
    *pieces, o_ref = refs
    logits = contract_blocks(x_ref, segments, win_ref, pieces, slice(None)) + b_ref[...]
    tracks = jax.nn.softplus(logits).astype(BF16)
    sums = jnp.dot(counts_ref[...], tracks, preferred_element_type=F32)
    o_ref[...] = sums.astype(o_ref.dtype)


def gene_counts(ranges, bins):
    position = jnp.arange(bins, dtype=jnp.int32)
    inside = (position >= ranges[0][:, :, None]) & (position < ranges[1][:, :, None])
    slots = jnp.arange(GENE_DEV, dtype=jnp.int32)
    chosen = ranges[2][:, None, :] == slots[None, :, None]
    counts = jnp.sum(
        (chosen[..., None] & inside[:, None]).astype(F32), axis=2
    )
    return counts.reshape(-1, bins).astype(BF16)


def local(
    feats,
    convolution_kernel_weight,
    conv_bias,
    qkv_weight,
    out_weight,
    head_weight,
    head_bias,
    exon_lists,
):
    segment_index = lax.axis_index("segment")
    win_index = lax.axis_index("win")
    model_index = lax.axis_index("mp")
    segments, windows, models = (lax.axis_size(a) for a in ("segment", "win", "mp"))
    chan_count, bin_count = feats.shape[1:]
    row_count, tap_count, out_cols = convolution_kernel_weight.shape
    bins = bin_count // segments
    reach = (tap_count - 1) // 2 * DILATION_STEP
    plane = ("segment", "mp")

    place = jnp.stack([segment_index, win_index, model_index]).astype(jnp.int32)

    def part_of_segment(*parts):
        width = sum(x.shape[1] for x in parts) // segments
        own = jax.ShapeDtypeStruct((row_count, width), BF16)
        return call_kernel(pack_kernel, own, place, *parts)

    attention_own = part_of_segment(qkv_weight, out_weight)
    head_cols = head_weight.shape[1] // segments
    head_own = lax.dynamic_slice_in_dim(head_weight, segment_index * head_cols, head_cols, 1)
    heads = qkv_weight.shape[1] // segments // SPAN
    stepwise = windows == 4 and models == 4

    def gathered(own, after, later):
        if not stepwise:
            return [lax.all_gather(own, "win", axis=0, tiled=True)]
        sent, _ = lax.optimization_barrier((own, after))
        below, above = shifted(sent, "win", 1), shifted(sent, "win", -1)
        handed = jnp.where(win_index == 1, above, jnp.where(win_index == 2, below, sent))
        handed, _ = lax.optimization_barrier((handed, later))
        across = lax.ppermute(handed, "win", [(0, 2), (1, 0), (2, 3), (3, 1)])
        return [own, below, across, above]

    win_ref = win_index.astype(jnp.int32)[None]
    track_cols = head_own.shape[1]
    bias_part = lax.dynamic_slice_in_dim(head_bias, segment_index * track_cols, track_cols, 0)
    counts = gene_counts(exon_lists[:, 0], bin_count)

    tap_weights = jnp.transpose(convolution_kernel_weight, (1, 0, 2))

    def conv_of(dtype, *operands):
        return call_kernel(
            conv_kernel if len(operands) == 1 else parts_conv_kernel,
            jax.ShapeDtypeStruct((bins, out_cols), dtype),
            *operands,
            tap_weights,
            flops=2 * bins * out_cols * row_count * tap_count,
        )

    if stepwise:
        block = jax.ShapeDtypeStruct((bins + 2 * reach, row_count), BF16)
        part = jax.ShapeDtypeStruct(((bins + 2 * reach) // 32 * 16 + 16, row_count), BF16)
        own_rows, next_rows, part_rows, own_feats = call_kernel(
            bins_kernel,
            [block, block, part, jax.ShapeDtypeStruct((bins, out_cols), BF16)],
            place,
            feats[0],
            scratch=[pltpu.VMEM((bin_count + 2 * reach, row_count), F32)],
        )

        def turned_by(x, even, odd):
            pairs = [
                (w * models + m, (w + (odd if m % 2 else even)) % windows * models + m)
                for w in range(windows)
                for m in range(models)
            ]
            return lax.ppermute(x, ("win", "mp"), pairs)

        def swapped(x):
            return lax.ppermute(x, "mp", [(m, m ^ 1) for m in range(models)])

        next_in, part_in = turned_by(next_rows, 1, -1), turned_by(part_rows, 2, 2)
        arrived = [next_in, part_in]
        swaps = [swapped(next_in), swapped(part_in)]
        conv_pre = conv_of(F32, own_rows)
        partials = [
            conv_of(BF16, next_in),
            conv_of(BF16, swaps[0]),
            conv_of(BF16, place, part_in, swaps[1]),
        ]
        returned = [
            turned_by(partials[0], -1, 1),
            turned_by(partials[1], 1, -1),
            turned_by(partials[2], 2, 2),
        ]
        attention_pieces = gathered(attention_own, arrived[0], returned[:2])
        for x in returned:
            conv_pre = conv_pre + x.astype(F32)
    else:
        padded = jnp.pad(feats[0].T, ((reach, reach), (0, 0)))
        own_bins = lax.dynamic_slice_in_dim(padded, segment_index * bins, bins + 2 * reach, 0)
        own_feats = lax.dynamic_slice(own_bins, (reach, model_index * out_cols), (bins, out_cols))
        blocks = own_bins.reshape(own_bins.shape[0], windows, row_count).transpose(1, 0, 2)
        arrived = lax.all_to_all(blocks, "win", 0, 0, tiled=True)
        attention_pieces = gathered(attention_own, None, None)
        partial = jnp.stack([conv_of(BF16, arrived[w]) for w in range(windows)])
        conv_pre = lax.all_to_all(partial, "win", 0, 0, tiled=True).astype(F32).sum(axis=0)

    conv_out = (own_feats + jax.nn.gelu(conv_pre + conv_bias)).astype(BF16)
    head_pieces = gathered(head_own, conv_out, ())
    all_chan = lax.all_gather(conv_out, plane, axis=0)

    partial = call_kernel(
        functools.partial(attention_kernel, segments, heads),
        jax.ShapeDtypeStruct(all_chan.shape, BF16),
        win_ref,
        all_chan,
        *attention_pieces,
    )
    summed = lax.all_to_all(partial, plane, 0, 0, tiled=True).astype(F32).sum(axis=0)
    resid = (conv_out.astype(F32) + summed).astype(BF16)
    all_resid = lax.all_gather(resid, plane, axis=0)

    sums = call_kernel(
        functools.partial(head_kernel, segments),
        jax.ShapeDtypeStruct((counts.shape[0], track_cols), BF16),
        win_ref,
        all_resid,
        bias_part[None, :],
        counts,
        *head_pieces,
    )
    owners = segments * windows
    got = lax.all_to_all(
        sums.reshape(owners, GENE_DEV, track_cols), ("segment", "win"), 0, 0, tiled=True
    )
    got = got.astype(F32).reshape(segments, windows, GENE_DEV, track_cols).sum(axis=1)
    return jnp.log1p(got.transpose(1, 0, 2).reshape(GENE_DEV, segments * track_cols))


def solution(mesh):
    in_specs = (
        P("win", None, None),
        P("win", None, "mp"),
        P("mp"),
        P("win", "mp"),
        P("win", "mp"),
        P("win", "mp"),
        P("mp"),
        P(None, "win", None, None),
    )
    out_specs = P(("segment", "win"), "mp")
    return jax.shard_map(local, mesh=mesh, in_specs=in_specs, out_specs=out_specs, check_vma=False)
```

```python
import functools
import math

import jax
import jax.numpy as jnp
from jax import lax
from jax.experimental import pallas as pl
from jax.experimental.pallas import tpu as pltpu
from jax.sharding import PartitionSpec as P

KEY = 64
VAL = 192
DILATION_STEP = 4
GENE_DEV = 8
SPAN = 2 * KEY + VAL
VMEM_BYTES = 40 * 1024 * 1024
F32 = jnp.float32
BF16 = jnp.bfloat16


def call_kernel(body, out_shape, *operands, scratch=(), flops=0):
    whole = pl.BlockSpec(memory_space=pltpu.VMEM)
    scalars = pl.BlockSpec(memory_space=pltpu.SMEM)
    return pl.pallas_call(
        body,
        out_shape=out_shape,
        in_specs=[scalars if x.dtype == jnp.int32 else whole for x in operands],
        out_specs=jax.tree.map(lambda _: whole, out_shape),
        scratch_shapes=list(scratch),
        compiler_params=pltpu.CompilerParams(vmem_limit_bytes=VMEM_BYTES),
        cost_estimate=pl.CostEstimate(flops=flops, bytes_accessed=1 << 20, transcendentals=0),
    )(*operands)


def shifted(x, axis, by):
    size = lax.axis_size(axis)
    return lax.ppermute(x, axis, [(i, (i + by) % size) for i in range(size)])


def bins_kernel(place_ref, x_ref, own_ref, next_ref, part_ref, rest_ref, padded):
    segment, window, model = place_ref[0], place_ref[1], place_ref[2]
    odd = lax.rem(model, 2)
    bins = rest_ref.shape[0]
    margin = (own_ref.shape[0] - bins) // 2
    start = segment * bins
    padded[:margin] = jnp.zeros((margin, padded.shape[1]), F32)
    padded[padded.shape[0] - margin :] = jnp.zeros((margin, padded.shape[1]), F32)

    def turned(block):
        first = pl.multiple_of(block * padded.shape[1], 16)
        columns = x_ref[pl.ds(first, padded.shape[1]), :].astype(F32)
        padded[margin : padded.shape[0] - margin] = columns.T

    def cut(out, first):
        out[...] = padded[pl.ds(pl.multiple_of(start + first, 8), out.shape[0])].astype(BF16)

    turned(lax.rem(window + 1 + 2 * odd, 4))
    cut(next_ref, 0)
    turned(lax.rem(window + 2, 4))
    cut(part_ref, odd * (own_ref.shape[0] - part_ref.shape[0]))
    turned(window)
    cut(own_ref, 0)
    turned(model)
    cut(rest_ref, margin)


def pack_kernel(place_ref, *refs):
    *parts, o_ref = refs
    segments = sum(x.shape[1] for x in parts) // o_ref.shape[1]
    for s in range(segments):

        @pl.when(place_ref[0] == s)
        def _():
            at = 0
            for x in parts:
                width = x.shape[1] // segments
                o_ref[:, at : at + width] = x[:, s * width : (s + 1) * width]
                at += width


def conv_kernel(x_ref, w_ref, o_ref):
    taps(x_ref[...].astype(F32), w_ref, o_ref)


def parts_conv_kernel(place_ref, own_ref, other_ref, w_ref, o_ref):
    even = lax.rem(place_ref[2], 2) == 0
    own, other = own_ref[...].astype(F32), other_ref[...].astype(F32)
    rows = o_ref.shape[0] + (w_ref.shape[0] - 1) * DILATION_STEP
    low = jnp.where(even, own, other)
    high = jnp.where(even, other, own)[2 * own.shape[0] - rows :]
    taps(jnp.concatenate([low, high], axis=0), w_ref, o_ref)


def taps(x, w_ref, o_ref):
    bins = o_ref.shape[0]
    total = jnp.zeros(o_ref.shape, F32)
    for tap in range(w_ref.shape[0]):
        start = tap * DILATION_STEP
        total += jnp.dot(
            x[start : start + bins].astype(BF16), w_ref[tap], preferred_element_type=F32
        )
    o_ref[...] = total.astype(o_ref.dtype)


def block_of(win_ref, by, windows):
    return lax.rem(win_ref[0] + windows - by, windows)


def contract_blocks(x_ref, segments, win_ref, pieces, cols):
    models = x_ref.shape[0] // segments
    total = None
    for by, piece in enumerate(pieces):
        if len(pieces) == 1:
            rows = [
                jnp.concatenate([x_ref[s * models + m] for m in range(models)], axis=1)
                for s in range(segments)
            ]
        else:
            block = block_of(win_ref, by, len(pieces))
            rows = [x_ref[s * models + block] for s in range(segments)]
        term = jnp.dot(jnp.concatenate(rows, axis=0), piece[:, cols], preferred_element_type=F32)
        total = term if total is None else total + term
    return total


def attention_kernel(segments, heads, place_ref, win_ref, x_ref, *refs):
    *pieces, keep_ref, give_ref = refs
    models = x_ref.shape[0] // segments
    bins, width = x_ref.shape[1:]
    rows = contract_blocks(x_ref, segments, win_ref, pieces, slice(0, heads * SPAN)).astype(BF16)
    outputs = []
    for head in range(heads):
        own = rows[:, head * SPAN : (head + 1) * SPAN]
        query, key, value = own[:, :KEY], own[:, KEY : 2 * KEY], own[:, 2 * KEY :]
        scores = lax.dot_general(
            query, key, (((1,), (1,)), ((), ())), preferred_element_type=F32
        ) * (1.0 / math.sqrt(KEY))
        weights = jnp.exp(scores)
        probs = (weights / jnp.sum(weights, axis=1, keepdims=True)).astype(BF16)
        outputs.append(jnp.dot(probs, value, preferred_element_type=F32).astype(BF16))
    att = jnp.concatenate(outputs, axis=1)
    odd = lax.rem(place_ref[2], 2)

    def put(segment, block, value):
        at = segment * (models // 2) + lax.div(block, 2)

        @pl.when(lax.rem(block, 2) == odd)
        def _():
            keep_ref[at] = value

        @pl.when(lax.rem(block, 2) != odd)
        def _():
            give_ref[at] = value

    for by, piece in enumerate(pieces):
        term = lax.dot_general(
            att,
            piece[:, heads * SPAN :],
            (((1,), (1,)), ((), ())),
            preferred_element_type=F32,
        ).astype(BF16)
        for s in range(segments):
            own = term[s * bins : (s + 1) * bins]
            if len(pieces) > 1:
                put(s, block_of(win_ref, by, len(pieces)), own)
            else:
                for m in range(models):
                    put(s, jnp.int32(m), own[:, m * width : (m + 1) * width])


def pair_kernel(place_ref, keep_ref, got_ref, *out_refs):
    segment, chip = place_ref[0], lax.div(place_ref[2], 2)
    for across, out in enumerate(out_refs):
        over_segment, over_mp = across % 2, across // 2
        at = (1 - segment if over_segment else segment) * 2 + (1 - chip if over_mp else chip)
        out[...] = (keep_ref[at].astype(F32) + got_ref[at].astype(F32)).astype(out.dtype)


def head_kernel(segments, win_ref, x_ref, b_ref, counts_ref, *refs):
    *pieces, o_ref = refs
    logits = contract_blocks(x_ref, segments, win_ref, pieces, slice(None)) + b_ref[...]
    tracks = jax.nn.softplus(logits).astype(BF16)
    sums = jnp.dot(counts_ref[...], tracks, preferred_element_type=F32)
    o_ref[...] = sums.astype(o_ref.dtype)


def gene_counts(ranges, bins):
    position = jnp.arange(bins, dtype=jnp.int32)
    inside = (position >= ranges[0][:, :, None]) & (position < ranges[1][:, :, None])
    slots = jnp.arange(GENE_DEV, dtype=jnp.int32)
    chosen = ranges[2][:, None, :] == slots[None, :, None]
    counts = jnp.sum(
        (chosen[..., None] & inside[:, None]).astype(F32), axis=2
    )
    return counts.reshape(-1, bins).astype(BF16)


def local(
    feats,
    convolution_kernel_weight,
    conv_bias,
    qkv_weight,
    out_weight,
    head_weight,
    head_bias,
    exon_lists,
):
    segment_index = lax.axis_index("segment")
    win_index = lax.axis_index("win")
    model_index = lax.axis_index("mp")
    segments, windows, models = (lax.axis_size(a) for a in ("segment", "win", "mp"))
    chan_count, bin_count = feats.shape[1:]
    row_count, tap_count, out_cols = convolution_kernel_weight.shape
    bins = bin_count // segments
    reach = (tap_count - 1) // 2 * DILATION_STEP
    plane = ("segment", "mp")

    place = jnp.stack([segment_index, win_index, model_index]).astype(jnp.int32)

    def part_of_segment(*parts):
        width = sum(x.shape[1] for x in parts) // segments
        own = jax.ShapeDtypeStruct((row_count, width), BF16)
        return call_kernel(pack_kernel, own, place, *parts)

    attention_own = part_of_segment(qkv_weight, out_weight)
    head_cols = head_weight.shape[1] // segments
    head_own = lax.dynamic_slice_in_dim(head_weight, segment_index * head_cols, head_cols, 1)
    heads = qkv_weight.shape[1] // segments // SPAN
    stepwise = windows == 4 and models == 4

    def gathered(own, after, later):
        if not stepwise:
            return [lax.all_gather(own, "win", axis=0, tiled=True)]
        sent, _ = lax.optimization_barrier((own, after))
        below, above = shifted(sent, "win", 1), shifted(sent, "win", -1)
        handed = jnp.where(win_index == 1, above, jnp.where(win_index == 2, below, sent))
        handed, _ = lax.optimization_barrier((handed, later))
        across = lax.ppermute(handed, "win", [(0, 2), (1, 0), (2, 3), (3, 1)])
        return [own, below, across, above]

    win_ref = win_index.astype(jnp.int32)[None]
    track_cols = head_own.shape[1]
    bias_part = lax.dynamic_slice_in_dim(head_bias, segment_index * track_cols, track_cols, 0)
    counts = gene_counts(exon_lists[:, 0], bin_count)

    tap_weights = jnp.transpose(convolution_kernel_weight, (1, 0, 2))

    def conv_of(dtype, *operands):
        return call_kernel(
            conv_kernel if len(operands) == 1 else parts_conv_kernel,
            jax.ShapeDtypeStruct((bins, out_cols), dtype),
            *operands,
            tap_weights,
            flops=2 * bins * out_cols * row_count * tap_count,
        )

    def swapped(x):
        return lax.ppermute(x, "mp", [(m, m ^ 1) for m in range(models)])

    if stepwise:
        block = jax.ShapeDtypeStruct((bins + 2 * reach, row_count), BF16)
        part = jax.ShapeDtypeStruct(((bins + 2 * reach) // 32 * 16 + 16, row_count), BF16)
        own_rows, next_rows, part_rows, own_feats = call_kernel(
            bins_kernel,
            [block, block, part, jax.ShapeDtypeStruct((bins, out_cols), BF16)],
            place,
            feats[0],
            scratch=[pltpu.VMEM((bin_count + 2 * reach, row_count), F32)],
        )

        def turned_by(x, even, odd):
            pairs = [
                (w * models + m, (w + (odd if m % 2 else even)) % windows * models + m)
                for w in range(windows)
                for m in range(models)
            ]
            return lax.ppermute(x, ("win", "mp"), pairs)

        next_in, part_in = turned_by(next_rows, 1, -1), turned_by(part_rows, 2, 2)
        arrived = [next_in, part_in]
        swaps = [swapped(next_in), swapped(part_in)]
        conv_pre = conv_of(F32, own_rows)
        partials = [
            conv_of(BF16, next_in),
            conv_of(BF16, swaps[0]),
            conv_of(BF16, place, part_in, swaps[1]),
        ]
        returned = [
            turned_by(partials[0], -1, 1),
            turned_by(partials[1], 1, -1),
            turned_by(partials[2], 2, 2),
        ]
        attention_pieces = gathered(attention_own, arrived[0], returned[:2])
        for x in returned:
            conv_pre = conv_pre + x.astype(F32)
    else:
        padded = jnp.pad(feats[0].T, ((reach, reach), (0, 0)))
        own_bins = lax.dynamic_slice_in_dim(padded, segment_index * bins, bins + 2 * reach, 0)
        own_feats = lax.dynamic_slice(own_bins, (reach, model_index * out_cols), (bins, out_cols))
        blocks = own_bins.reshape(own_bins.shape[0], windows, row_count).transpose(1, 0, 2)
        arrived = lax.all_to_all(blocks, "win", 0, 0, tiled=True)
        attention_pieces = gathered(attention_own, None, None)
        partial = jnp.stack([conv_of(BF16, arrived[w]) for w in range(windows)])
        conv_pre = lax.all_to_all(partial, "win", 0, 0, tiled=True).astype(F32).sum(axis=0)

    conv_out = (own_feats + jax.nn.gelu(conv_pre + conv_bias)).astype(BF16)
    head_pieces = gathered(head_own, conv_out, ())
    all_chan = lax.all_gather(conv_out, plane, axis=0)

    half = jax.ShapeDtypeStruct((segments * models // 2, bins, out_cols), BF16)
    keep, give = call_kernel(
        functools.partial(attention_kernel, segments, heads),
        [half, half],
        place,
        win_ref,
        all_chan,
        *attention_pieces,
    )
    one = jax.ShapeDtypeStruct((bins, out_cols), BF16)
    own_sum, *sent_sums = call_kernel(
        pair_kernel,
        [jax.ShapeDtypeStruct(one.shape, F32), one, one, one],
        place,
        keep,
        swapped(give),
    )
    summed = own_sum
    for across, x in enumerate(sent_sums, 1):
        pairs = [
            (s * models + m, (s ^ across % 2) * models + (m ^ across // 2 * 2))
            for s in range(segments)
            for m in range(models)
        ]
        summed = summed + lax.ppermute(x, plane, pairs).astype(F32)
    resid = (conv_out.astype(F32) + summed).astype(BF16)
    all_resid = lax.all_gather(resid, plane, axis=0)

    sums = call_kernel(
        functools.partial(head_kernel, segments),
        jax.ShapeDtypeStruct((counts.shape[0], track_cols), BF16),
        win_ref,
        all_resid,
        bias_part[None, :],
        counts,
        *head_pieces,
    )
    owners = segments * windows
    got = lax.all_to_all(
        sums.reshape(owners, GENE_DEV, track_cols), ("segment", "win"), 0, 0, tiled=True
    )
    got = got.astype(F32).reshape(segments, windows, GENE_DEV, track_cols).sum(axis=1)
    return jnp.log1p(got.transpose(1, 0, 2).reshape(GENE_DEV, segments * track_cols))


def solution(mesh):
    in_specs = (
        P("win", None, None),
        P("win", None, "mp"),
        P("mp"),
        P("win", "mp"),
        P("win", "mp"),
        P("win", "mp"),
        P("mp"),
        P(None, "win", None, None),
    )
    out_specs = P(("segment", "win"), "mp")
    return jax.shard_map(local, mesh=mesh, in_specs=in_specs, out_specs=out_specs, check_vma=False)
```

```python
import functools
import math

import jax
import jax.numpy as jnp
from jax import lax
from jax.experimental import pallas as pl
from jax.experimental.pallas import tpu as pltpu
from jax.sharding import PartitionSpec as P

KEY = 64
VAL = 192
DILATION_STEP = 4
GENE_DEV = 8
SPAN = 2 * KEY + VAL
VMEM_BYTES = 40 * 1024 * 1024
F32 = jnp.float32
BF16 = jnp.bfloat16


def call_kernel(body, out_shape, *operands, scratch=(), flops=0):
    whole = pl.BlockSpec(memory_space=pltpu.VMEM)
    scalars = pl.BlockSpec(memory_space=pltpu.SMEM)
    return pl.pallas_call(
        body,
        out_shape=out_shape,
        in_specs=[scalars if x.dtype == jnp.int32 else whole for x in operands],
        out_specs=jax.tree.map(lambda _: whole, out_shape),
        scratch_shapes=list(scratch),
        compiler_params=pltpu.CompilerParams(vmem_limit_bytes=VMEM_BYTES),
        cost_estimate=pl.CostEstimate(flops=flops, bytes_accessed=1 << 20, transcendentals=0),
    )(*operands)


def shifted(x, axis, by):
    size = lax.axis_size(axis)
    return lax.ppermute(x, axis, [(i, (i + by) % size) for i in range(size)])


def bins_kernel(place_ref, x_ref, own_ref, next_ref, part_ref, rest_ref, padded):
    segment, window, model = place_ref[0], place_ref[1], place_ref[2]
    odd = lax.rem(model, 2)
    bins = rest_ref.shape[0]
    margin = (own_ref.shape[0] - bins) // 2
    start = segment * bins
    padded[:margin] = jnp.zeros((margin, padded.shape[1]), F32)
    padded[padded.shape[0] - margin :] = jnp.zeros((margin, padded.shape[1]), F32)

    def turned(block):
        first = pl.multiple_of(block * padded.shape[1], 16)
        columns = x_ref[pl.ds(first, padded.shape[1]), :].astype(F32)
        padded[margin : padded.shape[0] - margin] = columns.T

    def cut(out, first):
        out[...] = padded[pl.ds(pl.multiple_of(start + first, 8), out.shape[0])].astype(BF16)

    turned(lax.rem(window + 1 + 2 * odd, 4))
    cut(next_ref, 0)
    turned(lax.rem(window + 2, 4))
    cut(part_ref, odd * (own_ref.shape[0] - part_ref.shape[0]))
    turned(window)
    cut(own_ref, 0)
    turned(model)
    cut(rest_ref, margin)


def turn_kernel(place_ref, x_ref, o_ref):
    width = o_ref.shape[0]
    for s in range(x_ref.shape[1] // width):

        @pl.when(place_ref[0] == s)
        def _():
            o_ref[...] = x_ref[:, s * width : (s + 1) * width].astype(F32).T.astype(BF16)


def conv_kernel(x_ref, w_ref, o_ref):
    taps(x_ref[...].astype(F32), w_ref, o_ref)


def parts_conv_kernel(place_ref, own_ref, other_ref, w_ref, o_ref):
    even = lax.rem(place_ref[2], 2) == 0
    own, other = own_ref[...].astype(F32), other_ref[...].astype(F32)
    rows = o_ref.shape[0] + (w_ref.shape[0] - 1) * DILATION_STEP
    low = jnp.where(even, own, other)
    high = jnp.where(even, other, own)[2 * own.shape[0] - rows :]
    taps(jnp.concatenate([low, high], axis=0), w_ref, o_ref)


def taps(x, w_ref, o_ref):
    bins = o_ref.shape[0]
    total = jnp.zeros(o_ref.shape, F32)
    for tap in range(w_ref.shape[0]):
        start = tap * DILATION_STEP
        total += jnp.dot(
            x[start : start + bins].astype(BF16), w_ref[tap], preferred_element_type=F32
        )
    o_ref[...] = total.astype(o_ref.dtype)


def block_of(win_ref, by, windows):
    return lax.rem(win_ref[0] + windows - by, windows)


def place_blocks(place_ref, refs, x_ref):
    segment, model = place_ref[0], place_ref[2]
    for at, ref in enumerate(refs):
        over_segment, over_mp = at % 2, at // 2
        s = 1 - segment if over_segment else segment
        pair = lax.div(model, 2)
        pair = 1 - pair if over_mp // 2 else pair
        odd = lax.rem(model, 2)
        odd = 1 - odd if over_mp % 2 else odd
        x_ref[s * 4 + pair * 2 + odd] = ref[...]


def block_rows(x_ref, segments, win_ref, by, pieces):
    models = x_ref.shape[0] // segments
    if pieces == 1:
        rows = [
            jnp.concatenate([x_ref[s * models + m] for m in range(models)], axis=1)
            for s in range(segments)
        ]
    else:
        block = block_of(win_ref, by, pieces)
        rows = [x_ref[s * models + block] for s in range(segments)]
    return jnp.concatenate(rows, axis=0)


def attention_kernel(segments, place_ref, win_ref, x_ref, *refs):
    *parts, keep_ref, give_ref = refs
    models = x_ref.shape[0] // segments
    bins, width = x_ref.shape[1:]
    if len(parts) == 2:
        qkv, out = [parts[0][...]], [parts[1][...]]
    else:
        *sides, across = parts
        qkv, out = ([x[...] for x in side] for side in (sides[:3], sides[3:]))
        qkv.insert(2, across[: qkv[0].shape[0]])
        out.insert(2, across[qkv[0].shape[0] :])
    heads = qkv[0].shape[0] // SPAN
    rows = None
    for by, piece in enumerate(qkv):
        term = lax.dot_general(
            block_rows(x_ref, segments, win_ref, by, len(qkv)),
            piece,
            (((1,), (1,)), ((), ())),
            preferred_element_type=F32,
        )
        rows = term if rows is None else rows + term
    rows = rows.astype(BF16)
    outputs = []
    for head in range(heads):
        own = rows[:, head * SPAN : (head + 1) * SPAN]
        query, key, value = own[:, :KEY], own[:, KEY : 2 * KEY], own[:, 2 * KEY :]
        scores = lax.dot_general(
            query, key, (((1,), (1,)), ((), ())), preferred_element_type=F32
        ) * (1.0 / math.sqrt(KEY))
        weights = jnp.exp(scores)
        probs = (weights / jnp.sum(weights, axis=1, keepdims=True)).astype(BF16)
        outputs.append(jnp.dot(probs, value, preferred_element_type=F32).astype(BF16))
    att = jnp.concatenate(outputs, axis=1)
    odd = lax.rem(place_ref[2], 2)

    def put(segment, block, value):
        at = segment * (models // 2) + lax.div(block, 2)

        @pl.when(lax.rem(block, 2) == odd)
        def _():
            keep_ref[at] = value

        @pl.when(lax.rem(block, 2) != odd)
        def _():
            give_ref[at] = value

    for by, piece in enumerate(out):
        term = jnp.dot(att, piece, preferred_element_type=F32).astype(BF16)
        for s in range(segments):
            own = term[s * bins : (s + 1) * bins]
            if len(out) > 1:
                put(s, block_of(win_ref, by, len(out)), own)
            else:
                for m in range(models):
                    put(s, jnp.int32(m), own[:, m * width : (m + 1) * width])


def pair_kernel(place_ref, keep_ref, got_ref, *out_refs):
    segment, chip = place_ref[0], lax.div(place_ref[2], 2)
    for across, out in enumerate(out_refs):
        over_segment, over_mp = across % 2, across // 2
        at = (1 - segment if over_segment else segment) * 2 + (1 - chip if over_mp else chip)
        out[...] = (keep_ref[at].astype(F32) + got_ref[at].astype(F32)).astype(out.dtype)


def head_kernel(segments, place_ref, win_ref, b_ref, counts_ref, *refs):
    blocks, (*pieces, o_ref, x_ref) = refs[:8], refs[8:]
    place_blocks(place_ref, blocks, x_ref)
    logits = b_ref[...]
    for by, piece in enumerate(pieces):
        rows = block_rows(x_ref, segments, win_ref, by, len(pieces))
        logits = logits + jnp.dot(rows, piece[...], preferred_element_type=F32)
    tracks = jax.nn.softplus(logits).astype(BF16)
    sums = jnp.dot(counts_ref[...], tracks, preferred_element_type=F32)
    o_ref[...] = sums.astype(o_ref.dtype)


def gene_counts(ranges, bins):
    position = jnp.arange(bins, dtype=jnp.int32)
    inside = (position >= ranges[0][:, :, None]) & (position < ranges[1][:, :, None])
    slots = jnp.arange(GENE_DEV, dtype=jnp.int32)
    chosen = ranges[2][:, None, :] == slots[None, :, None]
    counts = jnp.sum(
        (chosen[..., None] & inside[:, None]).astype(F32), axis=2
    )
    return counts.reshape(-1, bins).astype(BF16)


def local(
    feats,
    convolution_kernel_weight,
    conv_bias,
    qkv_weight,
    out_weight,
    head_weight,
    head_bias,
    exon_lists,
):
    segment_index = lax.axis_index("segment")
    win_index = lax.axis_index("win")
    model_index = lax.axis_index("mp")
    segments, windows, models = (lax.axis_size(a) for a in ("segment", "win", "mp"))
    chan_count, bin_count = feats.shape[1:]
    row_count, tap_count, out_cols = convolution_kernel_weight.shape
    bins = bin_count // segments
    reach = (tap_count - 1) // 2 * DILATION_STEP
    plane = ("segment", "mp")

    place = jnp.stack([segment_index, win_index, model_index]).astype(jnp.int32)

    def turned_part(x):
        own = jax.ShapeDtypeStruct((x.shape[1] // segments, row_count), BF16)
        return call_kernel(turn_kernel, own, place, x)

    qkv_own, out_own = turned_part(qkv_weight), turned_part(out_weight)
    head_cols = head_weight.shape[1] // segments
    head_own = lax.dynamic_slice_in_dim(head_weight, segment_index * head_cols, head_cols, 1)
    stepwise = windows == 4 and models == 4

    def first_stage(own, axis, *after):
        if not stepwise:
            return [lax.all_gather(own, "win", axis=axis, tiled=True)]
        return [own] + [
            shifted(lax.optimization_barrier((own, tie))[0], "win", by)
            for by, tie in zip((1, -1), after)
        ]

    def across(pieces, after):
        own, below, above = pieces
        handed = jnp.where(win_index == 1, above, jnp.where(win_index == 2, below, own))
        handed, _ = lax.optimization_barrier((handed, after))
        return lax.ppermute(handed, "win", [(0, 2), (1, 0), (2, 3), (3, 1)])

    win_ref = win_index.astype(jnp.int32)[None]
    track_cols = head_own.shape[1]
    bias_part = lax.dynamic_slice_in_dim(head_bias, segment_index * track_cols, track_cols, 0)
    counts = gene_counts(exon_lists[:, 0], bin_count)

    tap_weights = jnp.transpose(convolution_kernel_weight, (1, 0, 2))

    def conv_of(dtype, *operands):
        return call_kernel(
            conv_kernel if len(operands) == 1 else parts_conv_kernel,
            jax.ShapeDtypeStruct((bins, out_cols), dtype),
            *operands,
            tap_weights,
            flops=2 * bins * out_cols * row_count * tap_count,
        )

    def swapped(x):
        return lax.ppermute(x, "mp", [(m, m ^ 1) for m in range(models)])

    def over_plane(x, hop):
        pairs = [
            (s * models + m, (s ^ hop % 2) * models + (m ^ hop // 2 * 2))
            for s in range(segments)
            for m in range(models)
        ]
        return lax.ppermute(x, plane, pairs)

    def plane_blocks(x):
        same = [x] + [over_plane(x, hop) for hop in range(1, 4)]
        other = [swapped(b) for b in same]
        return [same[0], same[1], other[0], other[1], same[2], same[3], other[2], other[3]]

    all_blocks = [pltpu.VMEM((segments * models, bins, out_cols), BF16)]

    if stepwise:
        block = jax.ShapeDtypeStruct((bins + 2 * reach, row_count), BF16)
        part = jax.ShapeDtypeStruct(((bins + 2 * reach) // 32 * 16 + 16, row_count), BF16)
        own_rows, next_rows, part_rows, own_feats = call_kernel(
            bins_kernel,
            [block, block, part, jax.ShapeDtypeStruct((bins, out_cols), BF16)],
            place,
            feats[0],
            scratch=[pltpu.VMEM((bin_count + 2 * reach, row_count), F32)],
        )

        def turned_by(x, even, odd):
            pairs = [
                (w * models + m, (w + (odd if m % 2 else even)) % windows * models + m)
                for w in range(windows)
                for m in range(models)
            ]
            return lax.ppermute(x, ("win", "mp"), pairs)

        next_in, part_in = turned_by(next_rows, 1, -1), turned_by(part_rows, 2, 2)
        arrived = [next_in, part_in]
        swaps = [swapped(next_in), swapped(part_in)]
        conv_pre = conv_of(F32, own_rows)
        partials = [
            conv_of(BF16, next_in),
            conv_of(BF16, swaps[0]),
            conv_of(BF16, place, part_in, swaps[1]),
        ]
        returned = [
            turned_by(partials[0], -1, 1),
            turned_by(partials[1], 1, -1),
            turned_by(partials[2], 2, 2),
        ]
        qkv_pieces = first_stage(qkv_own, 1, arrived[0], arrived[0])
        out_pieces = first_stage(out_own, 1, (), ())
        both = [jnp.concatenate(x, axis=0) for x in zip(qkv_pieces, out_pieces)]
        attention_pieces = [*qkv_pieces, *out_pieces, across(both, returned[:2])]
        for x in returned:
            conv_pre = conv_pre + x.astype(F32)
    else:
        padded = jnp.pad(feats[0].T, ((reach, reach), (0, 0)))
        own_bins = lax.dynamic_slice_in_dim(padded, segment_index * bins, bins + 2 * reach, 0)
        own_feats = lax.dynamic_slice(own_bins, (reach, model_index * out_cols), (bins, out_cols))
        blocks = own_bins.reshape(own_bins.shape[0], windows, row_count).transpose(1, 0, 2)
        arrived = lax.all_to_all(blocks, "win", 0, 0, tiled=True)
        attention_pieces = first_stage(qkv_own, 1) + first_stage(out_own, 1)
        partial = jnp.stack([conv_of(BF16, arrived[w]) for w in range(windows)])
        conv_pre = lax.all_to_all(partial, "win", 0, 0, tiled=True).astype(F32).sum(axis=0)

    conv_out = (own_feats + jax.nn.gelu(conv_pre + conv_bias)).astype(BF16)
    head_pieces = first_stage(head_own, 0, conv_out, conv_out)
    if stepwise:
        head_pieces.insert(2, across(head_pieces, ()))
    all_chan = lax.all_gather(conv_out, plane, axis=0)

    half = jax.ShapeDtypeStruct((segments * models // 2, bins, out_cols), BF16)
    keep, give = call_kernel(
        functools.partial(attention_kernel, segments),
        [half, half],
        place,
        win_ref,
        all_chan,
        *attention_pieces,
    )
    one = jax.ShapeDtypeStruct((bins, out_cols), BF16)
    own_sum, *sent_sums = call_kernel(
        pair_kernel,
        [jax.ShapeDtypeStruct(one.shape, F32), one, one, one],
        place,
        keep,
        swapped(give),
    )
    summed = own_sum
    for hop, x in enumerate(sent_sums, 1):
        pairs = [
            (s * models + m, (s ^ hop % 2) * models + (m ^ hop // 2 * 2))
            for s in range(segments)
            for m in range(models)
        ]
        summed = summed + lax.ppermute(x, plane, pairs).astype(F32)
    resid = (conv_out.astype(F32) + summed).astype(BF16)
    all_resid = plane_blocks(resid)

    sums = call_kernel(
        functools.partial(head_kernel, segments),
        jax.ShapeDtypeStruct((counts.shape[0], track_cols), BF16),
        place,
        win_ref,
        bias_part[None, :],
        counts,
        *all_resid,
        *head_pieces,
        scratch=all_blocks,
    )
    owners = segments * windows
    got = lax.all_to_all(
        sums.reshape(owners, GENE_DEV, track_cols), ("segment", "win"), 0, 0, tiled=True
    )
    got = got.astype(F32).reshape(segments, windows, GENE_DEV, track_cols).sum(axis=1)
    return jnp.log1p(got.transpose(1, 0, 2).reshape(GENE_DEV, segments * track_cols))


def solution(mesh):
    in_specs = (
        P("win", None, None),
        P("win", None, "mp"),
        P("mp"),
        P("win", "mp"),
        P("win", "mp"),
        P("win", "mp"),
        P("mp"),
        P(None, "win", None, None),
    )
    out_specs = P(("segment", "win"), "mp")
    return jax.shard_map(local, mesh=mesh, in_specs=in_specs, out_specs=out_specs, check_vma=False)
```

```python
import functools
import math

import jax
import jax.numpy as jnp
from jax import lax
from jax.experimental import pallas as pl
from jax.experimental.pallas import tpu as pltpu
from jax.sharding import PartitionSpec as P

KEY = 64
VAL = 192
DILATION_STEP = 4
GENE_DEV = 8
SPAN = 2 * KEY + VAL
VMEM_BYTES = 40 * 1024 * 1024
F32 = jnp.float32
BF16 = jnp.bfloat16


def call_kernel(body, out_shape, *operands, scratch=(), flops=0):
    whole = pl.BlockSpec(memory_space=pltpu.VMEM)
    scalars = pl.BlockSpec(memory_space=pltpu.SMEM)
    return pl.pallas_call(
        body,
        out_shape=out_shape,
        in_specs=[scalars if x.dtype == jnp.int32 else whole for x in operands],
        out_specs=jax.tree.map(lambda _: whole, out_shape),
        scratch_shapes=list(scratch),
        compiler_params=pltpu.CompilerParams(vmem_limit_bytes=VMEM_BYTES),
        cost_estimate=pl.CostEstimate(flops=flops, bytes_accessed=1 << 20, transcendentals=0),
    )(*operands)


def shifted(x, axis, by):
    size = lax.axis_size(axis)
    return lax.ppermute(x, axis, [(i, (i + by) % size) for i in range(size)])


def bins_kernel(place_ref, x_ref, own_ref, next_ref, part_ref, rest_ref, padded):
    segment, window, model = place_ref[0], place_ref[1], place_ref[2]
    odd = lax.rem(model, 2)
    bins = rest_ref.shape[0]
    margin = (own_ref.shape[0] - bins) // 2
    start = segment * bins
    padded[:margin] = jnp.zeros((margin, padded.shape[1]), F32)
    padded[padded.shape[0] - margin :] = jnp.zeros((margin, padded.shape[1]), F32)

    def turned(block):
        first = pl.multiple_of(block * padded.shape[1], 16)
        columns = x_ref[pl.ds(first, padded.shape[1]), :].astype(F32)
        padded[margin : padded.shape[0] - margin] = columns.T

    def cut(out, first):
        out[...] = padded[pl.ds(pl.multiple_of(start + first, 8), out.shape[0])].astype(BF16)

    turned(lax.rem(window + 1 + 2 * odd, 4))
    cut(next_ref, 0)
    turned(lax.rem(window + 2, 4))
    cut(part_ref, odd * (own_ref.shape[0] - part_ref.shape[0]))
    turned(window)
    cut(own_ref, 0)
    turned(model)
    cut(rest_ref, margin)


def turn_kernel(place_ref, x_ref, o_ref):
    width = o_ref.shape[0]
    for s in range(x_ref.shape[1] // width):

        @pl.when(place_ref[0] == s)
        def _():
            o_ref[...] = x_ref[:, s * width : (s + 1) * width].astype(F32).T.astype(BF16)


def conv_kernel(x_ref, w_ref, o_ref):
    taps(x_ref[...].astype(F32), w_ref, o_ref)


def parts_conv_kernel(place_ref, own_ref, other_ref, w_ref, o_ref):
    even = lax.rem(place_ref[2], 2) == 0
    own, other = own_ref[...].astype(F32), other_ref[...].astype(F32)
    rows = o_ref.shape[0] + (w_ref.shape[0] - 1) * DILATION_STEP
    low = jnp.where(even, own, other)
    high = jnp.where(even, other, own)[2 * own.shape[0] - rows :]
    taps(jnp.concatenate([low, high], axis=0), w_ref, o_ref)


def taps(x, w_ref, o_ref):
    bins = o_ref.shape[0]
    total = jnp.zeros(o_ref.shape, F32)
    for tap in range(w_ref.shape[0]):
        start = tap * DILATION_STEP
        total += jnp.dot(
            x[start : start + bins].astype(BF16), w_ref[tap], preferred_element_type=F32
        )
    o_ref[...] = total.astype(o_ref.dtype)


def block_of(win_ref, by, windows):
    return lax.rem(win_ref[0] + windows - by, windows)


def place_blocks(place_ref, refs, x_ref):
    segment, model = place_ref[0], place_ref[2]
    for at, ref in enumerate(refs):
        over_segment, over_mp = at % 2, at // 2
        s = 1 - segment if over_segment else segment
        pair = lax.div(model, 2)
        pair = 1 - pair if over_mp // 2 else pair
        odd = lax.rem(model, 2)
        odd = 1 - odd if over_mp % 2 else odd
        x_ref[s * 4 + pair * 2 + odd] = ref[...]


def block_rows(x_ref, segments, win_ref, by, pieces):
    models = x_ref.shape[0] // segments
    if pieces == 1:
        rows = [
            jnp.concatenate([x_ref[s * models + m] for m in range(models)], axis=1)
            for s in range(segments)
        ]
    else:
        block = block_of(win_ref, by, pieces)
        rows = [x_ref[s * models + block] for s in range(segments)]
    return jnp.concatenate(rows, axis=0)


def attention_kernel(segments, place_ref, win_ref, x_ref, *refs):
    *parts, keep_ref, give_ref = refs
    models = x_ref.shape[0] // segments
    bins, width = x_ref.shape[1:]
    if len(parts) == 2:
        qkv, out = [parts[0][...]], [parts[1][...]]
    else:
        *sides, across = parts
        qkv, out = ([x[...] for x in side] for side in (sides[:3], sides[3:]))
        qkv.insert(2, across[: qkv[0].shape[0]])
        out.insert(2, across[qkv[0].shape[0] :])
    heads = qkv[0].shape[0] // SPAN
    rows = None
    for by, piece in enumerate(qkv):
        term = lax.dot_general(
            block_rows(x_ref, segments, win_ref, by, len(qkv)),
            piece,
            (((1,), (1,)), ((), ())),
            preferred_element_type=F32,
        )
        rows = term if rows is None else rows + term
    rows = rows.astype(BF16)
    outputs = []
    for head in range(heads):
        own = rows[:, head * SPAN : (head + 1) * SPAN]
        query, key, value = own[:, :KEY], own[:, KEY : 2 * KEY], own[:, 2 * KEY :]
        scores = lax.dot_general(
            query, key, (((1,), (1,)), ((), ())), preferred_element_type=F32
        ) * (1.0 / math.sqrt(KEY))
        weights = jnp.exp(scores)
        probs = (weights / jnp.sum(weights, axis=1, keepdims=True)).astype(BF16)
        outputs.append(jnp.dot(probs, value, preferred_element_type=F32).astype(BF16))
    att = jnp.concatenate(outputs, axis=1)
    odd = lax.rem(place_ref[2], 2)

    def put(segment, block, value):
        at = segment * (models // 2) + lax.div(block, 2)

        @pl.when(lax.rem(block, 2) == odd)
        def _():
            keep_ref[at] = value

        @pl.when(lax.rem(block, 2) != odd)
        def _():
            give_ref[at] = value

    for by, piece in enumerate(out):
        term = jnp.dot(att, piece, preferred_element_type=F32).astype(BF16)
        for s in range(segments):
            own = term[s * bins : (s + 1) * bins]
            if len(out) > 1:
                put(s, block_of(win_ref, by, len(out)), own)
            else:
                for m in range(models):
                    put(s, jnp.int32(m), own[:, m * width : (m + 1) * width])


def pair_kernel(place_ref, keep_ref, got_ref, *out_refs):
    segment, chip = place_ref[0], lax.div(place_ref[2], 2)
    for across, out in enumerate(out_refs):
        over_segment, over_mp = across % 2, across // 2
        at = (1 - segment if over_segment else segment) * 2 + (1 - chip if over_mp else chip)
        out[...] = (keep_ref[at].astype(F32) + got_ref[at].astype(F32)).astype(out.dtype)


def gene_sums(logits, b_ref, counts_ref, o_ref):
    tracks = jax.nn.softplus(logits + b_ref[...]).astype(BF16)
    sums = jnp.dot(counts_ref[...], tracks, preferred_element_type=F32)
    o_ref[...] = sums.astype(o_ref.dtype)


def head_kernel(segments, place_ref, win_ref, b_ref, counts_ref, *refs):
    blocks, (w_ref, o_ref, x_ref) = refs[:8], refs[8:]
    place_blocks(place_ref, blocks, x_ref)
    rows = block_rows(x_ref, segments, win_ref, 0, 1)
    gene_sums(jnp.dot(rows, w_ref[...], preferred_element_type=F32), b_ref, counts_ref, o_ref)


def near_head_kernel(segments, place_ref, win_ref, *refs):
    blocks, (own, below, above, logits_ref, rows_ref, x_ref) = refs[:8], refs[8:]
    place_blocks(place_ref, blocks, x_ref)
    logits = None
    for by, piece in ((0, own), (1, below), (3, above)):
        rows = block_rows(x_ref, segments, win_ref, by, 4)
        term = jnp.dot(rows, piece[...], preferred_element_type=F32)
        logits = term if logits is None else logits + term
    logits_ref[...] = logits
    rows_ref[...] = block_rows(x_ref, segments, win_ref, 2, 4)


def far_head_kernel(logits_ref, rows_ref, w_ref, b_ref, counts_ref, o_ref):
    term = jnp.dot(rows_ref[...], w_ref[...], preferred_element_type=F32)
    gene_sums(logits_ref[...] + term, b_ref, counts_ref, o_ref)


def gene_counts(ranges, bins):
    position = jnp.arange(bins, dtype=jnp.int32)
    inside = (position >= ranges[0][:, :, None]) & (position < ranges[1][:, :, None])
    slots = jnp.arange(GENE_DEV, dtype=jnp.int32)
    chosen = ranges[2][:, None, :] == slots[None, :, None]
    counts = jnp.sum(
        (chosen[..., None] & inside[:, None]).astype(F32), axis=2
    )
    return counts.reshape(-1, bins).astype(BF16)


def local(
    feats,
    convolution_kernel_weight,
    conv_bias,
    qkv_weight,
    out_weight,
    head_weight,
    head_bias,
    exon_lists,
):
    segment_index = lax.axis_index("segment")
    win_index = lax.axis_index("win")
    model_index = lax.axis_index("mp")
    segments, windows, models = (lax.axis_size(a) for a in ("segment", "win", "mp"))
    chan_count, bin_count = feats.shape[1:]
    row_count, tap_count, out_cols = convolution_kernel_weight.shape
    bins = bin_count // segments
    reach = (tap_count - 1) // 2 * DILATION_STEP
    plane = ("segment", "mp")

    place = jnp.stack([segment_index, win_index, model_index]).astype(jnp.int32)

    def turned_part(x):
        own = jax.ShapeDtypeStruct((x.shape[1] // segments, row_count), BF16)
        return call_kernel(turn_kernel, own, place, x)

    qkv_own, out_own = turned_part(qkv_weight), turned_part(out_weight)
    head_cols = head_weight.shape[1] // segments
    head_own = lax.dynamic_slice_in_dim(head_weight, segment_index * head_cols, head_cols, 1)
    stepwise = windows == 4 and models == 4

    def first_stage(own, axis, *after):
        if not stepwise:
            return [lax.all_gather(own, "win", axis=axis, tiled=True)]
        return [own] + [
            shifted(lax.optimization_barrier((own, tie))[0], "win", by)
            for by, tie in zip((1, -1), after)
        ]

    def across(pieces, after):
        own, below, above = pieces
        handed = jnp.where(win_index == 1, above, jnp.where(win_index == 2, below, own))
        handed, _ = lax.optimization_barrier((handed, after))
        return lax.ppermute(handed, "win", [(0, 2), (1, 0), (2, 3), (3, 1)])

    win_ref = win_index.astype(jnp.int32)[None]
    track_cols = head_own.shape[1]
    bias_part = lax.dynamic_slice_in_dim(head_bias, segment_index * track_cols, track_cols, 0)
    counts = gene_counts(exon_lists[:, 0], bin_count)

    tap_weights = jnp.transpose(convolution_kernel_weight, (1, 0, 2))

    def conv_of(dtype, *operands):
        return call_kernel(
            conv_kernel if len(operands) == 1 else parts_conv_kernel,
            jax.ShapeDtypeStruct((bins, out_cols), dtype),
            *operands,
            tap_weights,
            flops=2 * bins * out_cols * row_count * tap_count,
        )

    def swapped(x):
        return lax.ppermute(x, "mp", [(m, m ^ 1) for m in range(models)])

    def over_plane(x, hop):
        pairs = [
            (s * models + m, (s ^ hop % 2) * models + (m ^ hop // 2 * 2))
            for s in range(segments)
            for m in range(models)
        ]
        return lax.ppermute(x, plane, pairs)

    def plane_blocks(x):
        same = [x] + [over_plane(x, hop) for hop in range(1, 4)]
        other = [swapped(b) for b in same]
        return [same[0], same[1], other[0], other[1], same[2], same[3], other[2], other[3]]

    all_blocks = [pltpu.VMEM((segments * models, bins, out_cols), BF16)]

    if stepwise:
        block = jax.ShapeDtypeStruct((bins + 2 * reach, row_count), BF16)
        part = jax.ShapeDtypeStruct(((bins + 2 * reach) // 32 * 16 + 16, row_count), BF16)
        own_rows, next_rows, part_rows, own_feats = call_kernel(
            bins_kernel,
            [block, block, part, jax.ShapeDtypeStruct((bins, out_cols), BF16)],
            place,
            feats[0],
            scratch=[pltpu.VMEM((bin_count + 2 * reach, row_count), F32)],
        )

        def turned_by(x, even, odd):
            pairs = [
                (w * models + m, (w + (odd if m % 2 else even)) % windows * models + m)
                for w in range(windows)
                for m in range(models)
            ]
            return lax.ppermute(x, ("win", "mp"), pairs)

        next_in, part_in = turned_by(next_rows, 1, -1), turned_by(part_rows, 2, 2)
        arrived = [next_in, part_in]
        swaps = [swapped(next_in), swapped(part_in)]
        conv_pre = conv_of(F32, own_rows)
        partials = [
            conv_of(BF16, next_in),
            conv_of(BF16, swaps[0]),
            conv_of(BF16, place, part_in, swaps[1]),
        ]
        returned = [
            turned_by(partials[0], -1, 1),
            turned_by(partials[1], 1, -1),
            turned_by(partials[2], 2, 2),
        ]
        qkv_pieces = first_stage(qkv_own, 1, (), arrived[0])
        out_pieces = first_stage(out_own, 1, partials[0], partials[0])
        both = [jnp.concatenate(x, axis=0) for x in zip(qkv_pieces, out_pieces)]
        attention_pieces = [*qkv_pieces, *out_pieces, across(both, returned[1])]
        for x in returned:
            conv_pre = conv_pre + x.astype(F32)
    else:
        padded = jnp.pad(feats[0].T, ((reach, reach), (0, 0)))
        own_bins = lax.dynamic_slice_in_dim(padded, segment_index * bins, bins + 2 * reach, 0)
        own_feats = lax.dynamic_slice(own_bins, (reach, model_index * out_cols), (bins, out_cols))
        blocks = own_bins.reshape(own_bins.shape[0], windows, row_count).transpose(1, 0, 2)
        arrived = lax.all_to_all(blocks, "win", 0, 0, tiled=True)
        qkv_pieces = first_stage(qkv_own, 1)
        attention_pieces = qkv_pieces + first_stage(out_own, 1)
        partial = jnp.stack([conv_of(BF16, arrived[w]) for w in range(windows)])
        conv_pre = lax.all_to_all(partial, "win", 0, 0, tiled=True).astype(F32).sum(axis=0)

    conv_out = (own_feats + jax.nn.gelu(conv_pre + conv_bias)).astype(BF16)
    head_pieces = first_stage(head_own, 0, qkv_pieces[1:], conv_out)
    if stepwise:
        head_pieces.insert(2, across(head_pieces, ()))
    all_chan = lax.all_gather(conv_out, plane, axis=0)

    half = jax.ShapeDtypeStruct((segments * models // 2, bins, out_cols), BF16)
    keep, give = call_kernel(
        functools.partial(attention_kernel, segments),
        [half, half],
        place,
        win_ref,
        all_chan,
        *attention_pieces,
    )
    one = jax.ShapeDtypeStruct((bins, out_cols), BF16)
    own_sum, *sent_sums = call_kernel(
        pair_kernel,
        [jax.ShapeDtypeStruct(one.shape, F32), one, one, one],
        place,
        keep,
        swapped(give),
    )
    summed = own_sum
    for hop, x in enumerate(sent_sums, 1):
        pairs = [
            (s * models + m, (s ^ hop % 2) * models + (m ^ hop // 2 * 2))
            for s in range(segments)
            for m in range(models)
        ]
        summed = summed + lax.ppermute(x, plane, pairs).astype(F32)
    resid = (conv_out.astype(F32) + summed).astype(BF16)
    all_resid = plane_blocks(resid)

    sums_shape = jax.ShapeDtypeStruct((counts.shape[0], track_cols), BF16)
    if stepwise:
        own, below, far, above = head_pieces
        logits, far_rows = call_kernel(
            functools.partial(near_head_kernel, segments),
            [
                jax.ShapeDtypeStruct((bin_count, track_cols), F32),
                jax.ShapeDtypeStruct((bin_count, row_count), BF16),
            ],
            place,
            win_ref,
            *all_resid,
            own,
            below,
            above,
            scratch=all_blocks,
        )
        sums = call_kernel(
            far_head_kernel, sums_shape, logits, far_rows, far, bias_part[None, :], counts
        )
    else:
        sums = call_kernel(
            functools.partial(head_kernel, segments),
            sums_shape,
            place,
            win_ref,
            bias_part[None, :],
            counts,
            *all_resid,
            *head_pieces,
            scratch=all_blocks,
        )
    owners = segments * windows
    got = lax.all_to_all(
        sums.reshape(owners, GENE_DEV, track_cols), ("segment", "win"), 0, 0, tiled=True
    )
    got = got.astype(F32).reshape(segments, windows, GENE_DEV, track_cols).sum(axis=1)
    return jnp.log1p(got.transpose(1, 0, 2).reshape(GENE_DEV, segments * track_cols))


def solution(mesh):
    in_specs = (
        P("win", None, None),
        P("win", None, "mp"),
        P("mp"),
        P("win", "mp"),
        P("win", "mp"),
        P("win", "mp"),
        P("mp"),
        P(None, "win", None, None),
    )
    out_specs = P(("segment", "win"), "mp")
    return jax.shard_map(local, mesh=mesh, in_specs=in_specs, out_specs=out_specs, check_vma=False)
```

```python
import functools
import math

import jax
import jax.numpy as jnp
from jax import lax
from jax.experimental import pallas as pl
from jax.experimental.pallas import tpu as pltpu
from jax.sharding import PartitionSpec as P

KEY = 64
VAL = 192
DILATION_STEP = 4
GENE_DEV = 8
SPAN = 2 * KEY + VAL
VMEM_BYTES = 40 * 1024 * 1024
F32 = jnp.float32
BF16 = jnp.bfloat16


def call_kernel(body, out_shape, *operands, scratch=(), flops=0):
    whole = pl.BlockSpec(memory_space=pltpu.VMEM)
    scalars = pl.BlockSpec(memory_space=pltpu.SMEM)
    return pl.pallas_call(
        body,
        out_shape=out_shape,
        in_specs=[scalars if x.dtype == jnp.int32 else whole for x in operands],
        out_specs=jax.tree.map(lambda _: whole, out_shape),
        scratch_shapes=list(scratch),
        compiler_params=pltpu.CompilerParams(vmem_limit_bytes=VMEM_BYTES),
        cost_estimate=pl.CostEstimate(flops=flops, bytes_accessed=1 << 20, transcendentals=0),
    )(*operands)


def shifted(x, axis, by):
    size = lax.axis_size(axis)
    return lax.ppermute(x, axis, [(i, (i + by) % size) for i in range(size)])


def bins_kernel(place_ref, x_ref, own_ref, next_ref, part_ref, rest_ref, padded):
    segment, window, model = place_ref[0], place_ref[1], place_ref[2]
    odd = lax.rem(model, 2)
    bins = rest_ref.shape[0]
    margin = (own_ref.shape[0] - bins) // 2
    start = segment * bins
    padded[:margin] = jnp.zeros((margin, padded.shape[1]), F32)
    padded[padded.shape[0] - margin :] = jnp.zeros((margin, padded.shape[1]), F32)

    def turned(block):
        first = pl.multiple_of(block * padded.shape[1], 16)
        columns = x_ref[pl.ds(first, padded.shape[1]), :].astype(F32)
        padded[margin : padded.shape[0] - margin] = columns.T

    def cut(out, first):
        out[...] = padded[pl.ds(pl.multiple_of(start + first, 8), out.shape[0])].astype(BF16)

    turned(lax.rem(window + 1 + 2 * odd, 4))
    cut(next_ref, 0)
    turned(lax.rem(window + 2, 4))
    cut(part_ref, odd * (own_ref.shape[0] - part_ref.shape[0]))
    turned(window)
    cut(own_ref, 0)
    turned(model)
    cut(rest_ref, margin)


def turn_kernel(place_ref, x_ref, o_ref):
    width = o_ref.shape[0]
    for s in range(x_ref.shape[1] // width):

        @pl.when(place_ref[0] == s)
        def _():
            o_ref[...] = x_ref[:, s * width : (s + 1) * width].astype(F32).T.astype(BF16)


def conv_kernel(x_ref, w_ref, o_ref):
    taps(x_ref[...].astype(F32), w_ref, o_ref)


def parts_conv_kernel(place_ref, own_ref, other_ref, w_ref, o_ref):
    even = lax.rem(place_ref[2], 2) == 0
    own, other = own_ref[...].astype(F32), other_ref[...].astype(F32)
    rows = o_ref.shape[0] + (w_ref.shape[0] - 1) * DILATION_STEP
    low = jnp.where(even, own, other)
    high = jnp.where(even, other, own)[2 * own.shape[0] - rows :]
    taps(jnp.concatenate([low, high], axis=0), w_ref, o_ref)


def taps(x, w_ref, o_ref):
    bins = o_ref.shape[0]
    total = jnp.zeros(o_ref.shape, F32)
    for tap in range(w_ref.shape[0]):
        start = tap * DILATION_STEP
        total += jnp.dot(
            x[start : start + bins].astype(BF16), w_ref[tap], preferred_element_type=F32
        )
    o_ref[...] = total.astype(o_ref.dtype)


def block_of(win_ref, by, windows):
    return lax.rem(win_ref[0] + windows - by, windows)


def place_blocks(place_ref, refs, x_ref):
    segment, model = place_ref[0], place_ref[2]
    for at, ref in enumerate(refs):
        over_segment, over_mp = at % 2, at // 2
        s = 1 - segment if over_segment else segment
        pair = lax.div(model, 2)
        pair = 1 - pair if over_mp // 2 else pair
        odd = lax.rem(model, 2)
        odd = 1 - odd if over_mp % 2 else odd
        x_ref[s * 4 + pair * 2 + odd] = ref[...]


def block_rows(x_ref, segments, win_ref, by, pieces):
    models = x_ref.shape[0] // segments
    if pieces == 1:
        rows = [
            jnp.concatenate([x_ref[s * models + m] for m in range(models)], axis=1)
            for s in range(segments)
        ]
    else:
        block = block_of(win_ref, by, pieces)
        rows = [x_ref[s * models + block] for s in range(segments)]
    return jnp.concatenate(rows, axis=0)


def attention_kernel(segments, place_ref, win_ref, x_ref, *refs):
    *parts, keep_ref, give_ref = refs
    models = x_ref.shape[0] // segments
    bins, width = x_ref.shape[1:]
    if len(parts) == 2:
        qkv, out = [parts[0][...]], [parts[1][...]]
    else:
        *sides, across = parts
        qkv, out = ([x[...] for x in side] for side in (sides[:3], sides[3:]))
        qkv.insert(2, across[: qkv[0].shape[0]])
        out.insert(2, across[qkv[0].shape[0] :])
    heads = qkv[0].shape[0] // SPAN
    rows = None
    for by, piece in enumerate(qkv):
        term = lax.dot_general(
            block_rows(x_ref, segments, win_ref, by, len(qkv)),
            piece,
            (((1,), (1,)), ((), ())),
            preferred_element_type=F32,
        )
        rows = term if rows is None else rows + term
    rows = rows.astype(BF16)
    outputs = []
    for head in range(heads):
        own = rows[:, head * SPAN : (head + 1) * SPAN]
        query, key, value = own[:, :KEY], own[:, KEY : 2 * KEY], own[:, 2 * KEY :]
        scores = lax.dot_general(
            query, key, (((1,), (1,)), ((), ())), preferred_element_type=F32
        ) * (1.0 / math.sqrt(KEY))
        weights = jnp.exp(scores)
        probs = (weights / jnp.sum(weights, axis=1, keepdims=True)).astype(BF16)
        outputs.append(jnp.dot(probs, value, preferred_element_type=F32).astype(BF16))
    att = jnp.concatenate(outputs, axis=1)
    odd = lax.rem(place_ref[2], 2)

    def put(segment, block, value):
        at = segment * (models // 2) + lax.div(block, 2)

        @pl.when(lax.rem(block, 2) == odd)
        def _():
            keep_ref[at] = value

        @pl.when(lax.rem(block, 2) != odd)
        def _():
            give_ref[at] = value

    for by, piece in enumerate(out):
        term = jnp.dot(att, piece, preferred_element_type=F32).astype(BF16)
        for s in range(segments):
            own = term[s * bins : (s + 1) * bins]
            if len(out) > 1:
                put(s, block_of(win_ref, by, len(out)), own)
            else:
                for m in range(models):
                    put(s, jnp.int32(m), own[:, m * width : (m + 1) * width])


def pair_kernel(place_ref, keep_ref, got_ref, *out_refs):
    segment, chip = place_ref[0], lax.div(place_ref[2], 2)
    for across, out in enumerate(out_refs):
        over_segment, over_mp = across % 2, across // 2
        at = (1 - segment if over_segment else segment) * 2 + (1 - chip if over_mp else chip)
        out[...] = (keep_ref[at].astype(F32) + got_ref[at].astype(F32)).astype(out.dtype)


def gene_sums(logits, b_ref, counts_ref, o_ref):
    tracks = jax.nn.softplus(logits + b_ref[...]).astype(BF16)
    sums = jnp.dot(counts_ref[...], tracks, preferred_element_type=F32)
    o_ref[...] = sums.astype(o_ref.dtype)


def head_kernel(segments, place_ref, win_ref, b_ref, counts_ref, *refs):
    blocks, (w_ref, o_ref, x_ref) = refs[:8], refs[8:]
    place_blocks(place_ref, blocks, x_ref)
    rows = block_rows(x_ref, segments, win_ref, 0, 1)
    gene_sums(jnp.dot(rows, w_ref[...], preferred_element_type=F32), b_ref, counts_ref, o_ref)


def near_head_kernel(segments, place_ref, win_ref, *refs):
    blocks, (own, below, above, logits_ref, rows_ref, x_ref) = refs[:8], refs[8:]
    place_blocks(place_ref, blocks, x_ref)
    logits = None
    for by, piece in ((0, own), (1, below), (3, above)):
        rows = block_rows(x_ref, segments, win_ref, by, 4)
        term = jnp.dot(rows, piece[...], preferred_element_type=F32)
        logits = term if logits is None else logits + term
    logits_ref[...] = logits
    rows_ref[...] = block_rows(x_ref, segments, win_ref, 2, 4)


def far_head_kernel(logits_ref, rows_ref, w_ref, b_ref, counts_ref, o_ref):
    term = jnp.dot(rows_ref[...], w_ref[...], preferred_element_type=F32)
    gene_sums(logits_ref[...] + term, b_ref, counts_ref, o_ref)


def gene_counts(ranges, bins):
    position = jnp.arange(bins, dtype=jnp.int32)
    inside = (position >= ranges[0][:, :, None]) & (position < ranges[1][:, :, None])
    slots = jnp.arange(GENE_DEV, dtype=jnp.int32)
    chosen = ranges[2][:, None, :] == slots[None, :, None]
    counts = jnp.sum(
        (chosen[..., None] & inside[:, None]).astype(F32), axis=2
    )
    return counts.reshape(-1, bins).astype(BF16)


def local(
    feats,
    convolution_kernel_weight,
    conv_bias,
    qkv_weight,
    out_weight,
    head_weight,
    head_bias,
    exon_lists,
):
    segment_index = lax.axis_index("segment")
    win_index = lax.axis_index("win")
    model_index = lax.axis_index("mp")
    segments, windows, models = (lax.axis_size(a) for a in ("segment", "win", "mp"))
    chan_count, bin_count = feats.shape[1:]
    row_count, tap_count, out_cols = convolution_kernel_weight.shape
    bins = bin_count // segments
    reach = (tap_count - 1) // 2 * DILATION_STEP
    plane = ("segment", "mp")

    place = jnp.stack([segment_index, win_index, model_index]).astype(jnp.int32)

    def turned_part(x):
        own = jax.ShapeDtypeStruct((x.shape[1] // segments, row_count), BF16)
        return call_kernel(turn_kernel, own, place, x)

    qkv_own, out_own = turned_part(qkv_weight), turned_part(out_weight)
    head_cols = head_weight.shape[1] // segments
    head_own = lax.dynamic_slice_in_dim(head_weight, segment_index * head_cols, head_cols, 1)
    stepwise = windows == 4 and models == 4

    def first_stage(own, axis, *after):
        if not stepwise:
            return [lax.all_gather(own, "win", axis=axis, tiled=True)]
        return [own] + [
            shifted(lax.optimization_barrier((own, tie))[0], "win", by)
            for by, tie in zip((1, -1), after)
        ]

    def across(pieces, after):
        own, below, above = pieces
        handed = jnp.where(win_index == 1, above, jnp.where(win_index == 2, below, own))
        handed, _ = lax.optimization_barrier((handed, after))
        return lax.ppermute(handed, "win", [(0, 2), (1, 0), (2, 3), (3, 1)])

    win_ref = win_index.astype(jnp.int32)[None]
    track_cols = head_own.shape[1]
    bias_part = lax.dynamic_slice_in_dim(head_bias, segment_index * track_cols, track_cols, 0)

    tap_weights = jnp.transpose(convolution_kernel_weight, (1, 0, 2))

    def conv_of(dtype, *operands):
        return call_kernel(
            conv_kernel if len(operands) == 1 else parts_conv_kernel,
            jax.ShapeDtypeStruct((bins, out_cols), dtype),
            *operands,
            tap_weights,
            flops=2 * bins * out_cols * row_count * tap_count,
        )

    def swapped(x):
        return lax.ppermute(x, "mp", [(m, m ^ 1) for m in range(models)])

    def over_plane(x, hop):
        pairs = [
            (s * models + m, (s ^ hop % 2) * models + (m ^ hop // 2 * 2))
            for s in range(segments)
            for m in range(models)
        ]
        return lax.ppermute(x, plane, pairs)

    def plane_blocks(x):
        same = [x] + [over_plane(x, hop) for hop in range(1, 4)]
        other = [swapped(b) for b in same]
        return [same[0], same[1], other[0], other[1], same[2], same[3], other[2], other[3]]

    all_blocks = [pltpu.VMEM((segments * models, bins, out_cols), BF16)]

    if stepwise:
        block = jax.ShapeDtypeStruct((bins + 2 * reach, row_count), BF16)
        part = jax.ShapeDtypeStruct(((bins + 2 * reach) // 32 * 16 + 16, row_count), BF16)
        own_rows, next_rows, part_rows, own_feats = call_kernel(
            bins_kernel,
            [block, block, part, jax.ShapeDtypeStruct((bins, out_cols), BF16)],
            place,
            feats[0],
            scratch=[pltpu.VMEM((bin_count + 2 * reach, row_count), F32)],
        )

        def turned_by(x, even, odd):
            pairs = [
                (w * models + m, (w + (odd if m % 2 else even)) % windows * models + m)
                for w in range(windows)
                for m in range(models)
            ]
            return lax.ppermute(x, ("win", "mp"), pairs)

        next_in, part_in = turned_by(next_rows, 1, -1), turned_by(part_rows, 2, 2)
        arrived = [next_in, part_in]
        swaps = [swapped(next_in), swapped(part_in)]
        partials = [
            conv_of(BF16, next_in),
            conv_of(BF16, swaps[0]),
            conv_of(BF16, place, part_in, swaps[1]),
        ]
        late_rows, _ = lax.optimization_barrier((own_rows, partials))
        conv_pre = conv_of(F32, late_rows)
        returned = [
            turned_by(partials[0], -1, 1),
            turned_by(partials[1], 1, -1),
            turned_by(partials[2], 2, 2),
        ]
        qkv_pieces = first_stage(qkv_own, 1, (), arrived[0])
        out_pieces = first_stage(out_own, 1, arrived[0], partials[0])
        both = [jnp.concatenate(x, axis=0) for x in zip(qkv_pieces, out_pieces)]
        attention_pieces = [*qkv_pieces, *out_pieces, across(both, returned[1])]
        for x in returned:
            conv_pre = conv_pre + x.astype(F32)
    else:
        padded = jnp.pad(feats[0].T, ((reach, reach), (0, 0)))
        own_bins = lax.dynamic_slice_in_dim(padded, segment_index * bins, bins + 2 * reach, 0)
        own_feats = lax.dynamic_slice(own_bins, (reach, model_index * out_cols), (bins, out_cols))
        blocks = own_bins.reshape(own_bins.shape[0], windows, row_count).transpose(1, 0, 2)
        arrived = lax.all_to_all(blocks, "win", 0, 0, tiled=True)
        qkv_pieces = first_stage(qkv_own, 1)
        attention_pieces = qkv_pieces + first_stage(out_own, 1)
        partial = jnp.stack([conv_of(BF16, arrived[w]) for w in range(windows)])
        conv_pre = lax.all_to_all(partial, "win", 0, 0, tiled=True).astype(F32).sum(axis=0)

    conv_out = (own_feats + jax.nn.gelu(conv_pre + conv_bias)).astype(BF16)
    head_pieces = first_stage(head_own, 0, qkv_pieces[1:], conv_out)
    if stepwise:
        head_pieces.insert(2, across(head_pieces, ()))
    all_chan = lax.all_gather(conv_out, plane, axis=0)
    lists, _ = lax.optimization_barrier((exon_lists[:, 0], conv_out))
    counts = gene_counts(lists, bin_count)

    half = jax.ShapeDtypeStruct((segments * models // 2, bins, out_cols), BF16)
    keep, give = call_kernel(
        functools.partial(attention_kernel, segments),
        [half, half],
        place,
        win_ref,
        all_chan,
        *attention_pieces,
    )
    one = jax.ShapeDtypeStruct((bins, out_cols), BF16)
    own_sum, *sent_sums = call_kernel(
        pair_kernel,
        [jax.ShapeDtypeStruct(one.shape, F32), one, one, one],
        place,
        keep,
        swapped(give),
    )
    summed = own_sum
    for hop, x in enumerate(sent_sums, 1):
        pairs = [
            (s * models + m, (s ^ hop % 2) * models + (m ^ hop // 2 * 2))
            for s in range(segments)
            for m in range(models)
        ]
        summed = summed + lax.ppermute(x, plane, pairs).astype(F32)
    resid = (conv_out.astype(F32) + summed).astype(BF16)
    all_resid = plane_blocks(resid)

    sums_shape = jax.ShapeDtypeStruct((counts.shape[0], track_cols), BF16)
    if stepwise:
        own, below, far, above = head_pieces
        logits, far_rows = call_kernel(
            functools.partial(near_head_kernel, segments),
            [
                jax.ShapeDtypeStruct((bin_count, track_cols), F32),
                jax.ShapeDtypeStruct((bin_count, row_count), BF16),
            ],
            place,
            win_ref,
            *all_resid,
            own,
            below,
            above,
            scratch=all_blocks,
        )
        sums = call_kernel(
            far_head_kernel, sums_shape, logits, far_rows, far, bias_part[None, :], counts
        )
    else:
        sums = call_kernel(
            functools.partial(head_kernel, segments),
            sums_shape,
            place,
            win_ref,
            bias_part[None, :],
            counts,
            *all_resid,
            *head_pieces,
            scratch=all_blocks,
        )
    owners = segments * windows
    got = lax.all_to_all(
        sums.reshape(owners, GENE_DEV, track_cols), ("segment", "win"), 0, 0, tiled=True
    )
    got = got.astype(F32).reshape(segments, windows, GENE_DEV, track_cols).sum(axis=1)
    return jnp.log1p(got.transpose(1, 0, 2).reshape(GENE_DEV, segments * track_cols))


def solution(mesh):
    in_specs = (
        P("win", None, None),
        P("win", None, "mp"),
        P("mp"),
        P("win", "mp"),
        P("win", "mp"),
        P("win", "mp"),
        P("mp"),
        P(None, "win", None, None),
    )
    out_specs = P(("segment", "win"), "mp")
    return jax.shard_map(local, mesh=mesh, in_specs=in_specs, out_specs=out_specs, check_vma=False)
```

```python
import functools
import math

import jax
import jax.numpy as jnp
from jax import lax
from jax.experimental import pallas as pl
from jax.experimental.pallas import tpu as pltpu
from jax.sharding import PartitionSpec as P

KEY = 64
VAL = 192
DILATION_STEP = 4
GENE_DEV = 8
SPAN = 2 * KEY + VAL
VMEM_BYTES = 40 * 1024 * 1024
F32 = jnp.float32
BF16 = jnp.bfloat16


def call_kernel(body, out_shape, *operands, scratch=(), flops=0):
    whole = pl.BlockSpec(memory_space=pltpu.VMEM)
    scalars = pl.BlockSpec(memory_space=pltpu.SMEM)
    return pl.pallas_call(
        body,
        out_shape=out_shape,
        in_specs=[scalars if x.dtype == jnp.int32 else whole for x in operands],
        out_specs=jax.tree.map(lambda _: whole, out_shape),
        scratch_shapes=list(scratch),
        compiler_params=pltpu.CompilerParams(vmem_limit_bytes=VMEM_BYTES),
        cost_estimate=pl.CostEstimate(flops=flops, bytes_accessed=1 << 20, transcendentals=0),
    )(*operands)


def shifted(x, axis, by):
    size = lax.axis_size(axis)
    return lax.ppermute(x, axis, [(i, (i + by) % size) for i in range(size)])


def bins_kernel(place_ref, x_ref, own_ref, next_ref, part_ref, rest_ref, padded):
    segment, window, model = place_ref[0], place_ref[1], place_ref[2]
    odd = lax.rem(model, 2)
    bins = rest_ref.shape[0]
    margin = (own_ref.shape[0] - bins) // 2
    start = segment * bins
    padded[:margin] = jnp.zeros((margin, padded.shape[1]), F32)
    padded[padded.shape[0] - margin :] = jnp.zeros((margin, padded.shape[1]), F32)

    def turned(block):
        first = pl.multiple_of(block * padded.shape[1], 16)
        columns = x_ref[pl.ds(first, padded.shape[1]), :].astype(F32)
        padded[margin : padded.shape[0] - margin] = columns.T

    def cut(out, first):
        out[...] = padded[pl.ds(pl.multiple_of(start + first, 8), out.shape[0])].astype(BF16)

    turned(lax.rem(window + 1 + 2 * odd, 4))
    cut(next_ref, 0)
    turned(lax.rem(window + 2, 4))
    cut(part_ref, odd * (own_ref.shape[0] - part_ref.shape[0]))
    turned(window)
    cut(own_ref, 0)
    turned(model)
    cut(rest_ref, margin)


def turn_kernel(place_ref, x_ref, o_ref):
    width = o_ref.shape[0]
    for s in range(x_ref.shape[1] // width):

        @pl.when(place_ref[0] == s)
        def _():
            o_ref[...] = x_ref[:, s * width : (s + 1) * width].astype(F32).T.astype(BF16)


def conv_kernel(x_ref, w_ref, o_ref):
    taps(x_ref[...].astype(F32), w_ref, o_ref)


def parts_conv_kernel(place_ref, own_ref, other_ref, w_ref, o_ref):
    even = lax.rem(place_ref[2], 2) == 0
    own, other = own_ref[...].astype(F32), other_ref[...].astype(F32)
    rows = o_ref.shape[0] + (w_ref.shape[0] - 1) * DILATION_STEP
    low = jnp.where(even, own, other)
    high = jnp.where(even, other, own)[2 * own.shape[0] - rows :]
    taps(jnp.concatenate([low, high], axis=0), w_ref, o_ref)


def taps(x, w_ref, o_ref):
    bins = o_ref.shape[0]
    total = jnp.zeros(o_ref.shape, F32)
    for tap in range(w_ref.shape[0]):
        start = tap * DILATION_STEP
        total += jnp.dot(
            x[start : start + bins].astype(BF16), w_ref[tap], preferred_element_type=F32
        )
    o_ref[...] = total.astype(o_ref.dtype)


def block_of(win_ref, by, windows):
    return lax.rem(win_ref[0] + windows - by, windows)


def place_blocks(place_ref, refs, x_ref):
    segment, model = place_ref[0], place_ref[2]
    for at, ref in enumerate(refs):
        over_segment, over_mp = at % 2, at // 2
        s = 1 - segment if over_segment else segment
        pair = lax.div(model, 2)
        pair = 1 - pair if over_mp // 2 else pair
        odd = lax.rem(model, 2)
        odd = 1 - odd if over_mp % 2 else odd
        x_ref[s * 4 + pair * 2 + odd] = ref[...]


def block_rows(x_ref, segments, win_ref, by, pieces):
    models = x_ref.shape[0] // segments
    if pieces == 1:
        rows = [
            jnp.concatenate([x_ref[s * models + m] for m in range(models)], axis=1)
            for s in range(segments)
        ]
    else:
        block = block_of(win_ref, by, pieces)
        rows = [x_ref[s * models + block] for s in range(segments)]
    return jnp.concatenate(rows, axis=0)


def attention_kernel(segments, place_ref, win_ref, x_ref, *refs):
    *parts, keep_ref, give_ref = refs
    models = x_ref.shape[0] // segments
    bins, width = x_ref.shape[1:]
    if len(parts) == 2:
        qkv, out = [parts[0][...]], [parts[1][...]]
    else:
        *sides, across = parts
        qkv, out = ([x[...] for x in side] for side in (sides[:3], sides[3:]))
        qkv.insert(2, across[: qkv[0].shape[0]])
        out.insert(2, across[qkv[0].shape[0] :])
    heads = qkv[0].shape[0] // SPAN
    rows = None
    for by, piece in enumerate(qkv):
        term = lax.dot_general(
            block_rows(x_ref, segments, win_ref, by, len(qkv)),
            piece,
            (((1,), (1,)), ((), ())),
            preferred_element_type=F32,
        )
        rows = term if rows is None else rows + term
    rows = rows.astype(BF16)
    outputs = []
    for head in range(heads):
        own = rows[:, head * SPAN : (head + 1) * SPAN]
        query, key, value = own[:, :KEY], own[:, KEY : 2 * KEY], own[:, 2 * KEY :]
        scores = lax.dot_general(
            query, key, (((1,), (1,)), ((), ())), preferred_element_type=F32
        ) * (1.0 / math.sqrt(KEY))
        weights = jnp.exp(scores)
        probs = (weights / jnp.sum(weights, axis=1, keepdims=True)).astype(BF16)
        outputs.append(jnp.dot(probs, value, preferred_element_type=F32).astype(BF16))
    att = jnp.concatenate(outputs, axis=1)
    odd = lax.rem(place_ref[2], 2)

    def put(segment, block, value):
        at = segment * (models // 2) + lax.div(block, 2)

        @pl.when(lax.rem(block, 2) == odd)
        def _():
            keep_ref[at] = value

        @pl.when(lax.rem(block, 2) != odd)
        def _():
            give_ref[at] = value

    for by, piece in enumerate(out):
        term = jnp.dot(att, piece, preferred_element_type=F32).astype(BF16)
        for s in range(segments):
            own = term[s * bins : (s + 1) * bins]
            if len(out) > 1:
                put(s, block_of(win_ref, by, len(out)), own)
            else:
                for m in range(models):
                    put(s, jnp.int32(m), own[:, m * width : (m + 1) * width])


def pair_kernel(place_ref, keep_ref, got_ref, *out_refs):
    segment, chip = place_ref[0], lax.div(place_ref[2], 2)
    for across, out in enumerate(out_refs):
        over_segment, over_mp = across % 2, across // 2
        at = (1 - segment if over_segment else segment) * 2 + (1 - chip if over_mp else chip)
        out[...] = (keep_ref[at].astype(F32) + got_ref[at].astype(F32)).astype(out.dtype)


def gene_sums(logits, b_ref, counts_ref, o_ref):
    tracks = jax.nn.softplus(logits + b_ref[...]).astype(BF16)
    sums = jnp.dot(counts_ref[...], tracks, preferred_element_type=F32)
    o_ref[...] = sums.astype(o_ref.dtype)


def head_kernel(segments, place_ref, win_ref, b_ref, counts_ref, *refs):
    blocks, (w_ref, o_ref, x_ref) = refs[:8], refs[8:]
    place_blocks(place_ref, blocks, x_ref)
    rows = block_rows(x_ref, segments, win_ref, 0, 1)
    gene_sums(jnp.dot(rows, w_ref[...], preferred_element_type=F32), b_ref, counts_ref, o_ref)


def near_head_kernel(segments, place_ref, win_ref, *refs):
    blocks, (own, below, above, logits_ref, rows_ref, x_ref) = refs[:8], refs[8:]
    place_blocks(place_ref, blocks, x_ref)
    logits = None
    for by, piece in ((0, own), (1, below), (3, above)):
        rows = block_rows(x_ref, segments, win_ref, by, 4)
        term = jnp.dot(rows, piece[...], preferred_element_type=F32)
        logits = term if logits is None else logits + term
    logits_ref[...] = logits
    rows_ref[...] = block_rows(x_ref, segments, win_ref, 2, 4)


def far_head_kernel(logits_ref, rows_ref, w_ref, b_ref, counts_ref, o_ref):
    term = jnp.dot(rows_ref[...], w_ref[...], preferred_element_type=F32)
    gene_sums(logits_ref[...] + term, b_ref, counts_ref, o_ref)


def gene_counts(ranges, bins):
    position = jnp.arange(bins, dtype=jnp.int32)
    inside = (position >= ranges[0][:, :, None]) & (position < ranges[1][:, :, None])
    slots = jnp.arange(GENE_DEV, dtype=jnp.int32)
    chosen = ranges[2][:, None, :] == slots[None, :, None]
    counts = jnp.sum(
        (chosen[..., None] & inside[:, None]).astype(F32), axis=2
    )
    return counts.reshape(-1, bins).astype(BF16)


def local(
    feats,
    convolution_kernel_weight,
    conv_bias,
    qkv_weight,
    out_weight,
    head_weight,
    head_bias,
    exon_lists,
):
    segment_index = lax.axis_index("segment")
    win_index = lax.axis_index("win")
    model_index = lax.axis_index("mp")
    segments, windows, models = (lax.axis_size(a) for a in ("segment", "win", "mp"))
    chan_count, bin_count = feats.shape[1:]
    row_count, tap_count, out_cols = convolution_kernel_weight.shape
    bins = bin_count // segments
    reach = (tap_count - 1) // 2 * DILATION_STEP
    plane = ("segment", "mp")

    place = jnp.stack([segment_index, win_index, model_index]).astype(jnp.int32)

    def turned_part(x):
        own = jax.ShapeDtypeStruct((x.shape[1] // segments, row_count), BF16)
        return call_kernel(turn_kernel, own, place, x)

    qkv_own, out_own = turned_part(qkv_weight), turned_part(out_weight)
    head_cols = head_weight.shape[1] // segments
    head_own = lax.dynamic_slice_in_dim(head_weight, segment_index * head_cols, head_cols, 1)
    stepwise = windows == 4 and models == 4

    def first_stage(own, axis, *after):
        if not stepwise:
            return [lax.all_gather(own, "win", axis=axis, tiled=True)]
        return [own] + [
            shifted(lax.optimization_barrier((own, tie))[0], "win", by)
            for by, tie in zip((1, -1), after)
        ]

    def across(pieces, after):
        own, below, above = pieces
        handed = jnp.where(win_index == 1, above, jnp.where(win_index == 2, below, own))
        handed, _ = lax.optimization_barrier((handed, after))
        return lax.ppermute(handed, "win", [(0, 2), (1, 0), (2, 3), (3, 1)])

    win_ref = win_index.astype(jnp.int32)[None]
    track_cols = head_own.shape[1]
    bias_part = lax.dynamic_slice_in_dim(head_bias, segment_index * track_cols, track_cols, 0)

    tap_weights = jnp.transpose(convolution_kernel_weight, (1, 0, 2))

    def conv_of(dtype, *operands):
        return call_kernel(
            conv_kernel if len(operands) == 1 else parts_conv_kernel,
            jax.ShapeDtypeStruct((bins, out_cols), dtype),
            *operands,
            tap_weights,
            flops=2 * bins * out_cols * row_count * tap_count,
        )

    def swapped(x):
        return lax.ppermute(x, "mp", [(m, m ^ 1) for m in range(models)])

    def over_plane(x, hop):
        pairs = [
            (s * models + m, (s ^ hop % 2) * models + (m ^ hop // 2 * 2))
            for s in range(segments)
            for m in range(models)
        ]
        return lax.ppermute(x, plane, pairs)

    def plane_blocks(x):
        same = [x] + [over_plane(x, hop) for hop in range(1, 4)]
        other = [swapped(b) for b in same]
        return [same[0], same[1], other[0], other[1], same[2], same[3], other[2], other[3]]

    all_blocks = [pltpu.VMEM((segments * models, bins, out_cols), BF16)]

    if stepwise:
        block = jax.ShapeDtypeStruct((bins + 2 * reach, row_count), BF16)
        part = jax.ShapeDtypeStruct(((bins + 2 * reach) // 32 * 16 + 16, row_count), BF16)
        own_rows, next_rows, part_rows, own_feats = call_kernel(
            bins_kernel,
            [block, block, part, jax.ShapeDtypeStruct((bins, out_cols), BF16)],
            place,
            feats[0],
            scratch=[pltpu.VMEM((bin_count + 2 * reach, row_count), F32)],
        )

        def turned_by(x, even, odd):
            pairs = [
                (w * models + m, (w + (odd if m % 2 else even)) % windows * models + m)
                for w in range(windows)
                for m in range(models)
            ]
            return lax.ppermute(x, ("win", "mp"), pairs)

        next_in, part_in = turned_by(next_rows, 1, -1), turned_by(part_rows, 2, 2)
        arrived = [next_in, part_in]
        swaps = [swapped(next_in), swapped(part_in)]
        partials = [
            conv_of(BF16, next_in),
            conv_of(BF16, swaps[0]),
            conv_of(BF16, place, part_in, swaps[1]),
        ]
        late_rows, _ = lax.optimization_barrier((own_rows, partials))
        conv_pre = conv_of(F32, late_rows)
        returned = [
            turned_by(partials[0], -1, 1),
            turned_by(partials[1], 1, -1),
            turned_by(partials[2], 2, 2),
        ]
        qkv_pieces = first_stage(qkv_own, 1, (), arrived[0])
        out_pieces = first_stage(out_own, 1, arrived[0], ())
        both = [jnp.concatenate(x, axis=0) for x in zip(qkv_pieces, out_pieces)]
        attention_pieces = [*qkv_pieces, *out_pieces, across(both, returned[:2])]
        for x in returned:
            conv_pre = conv_pre + x.astype(F32)
    else:
        padded = jnp.pad(feats[0].T, ((reach, reach), (0, 0)))
        own_bins = lax.dynamic_slice_in_dim(padded, segment_index * bins, bins + 2 * reach, 0)
        own_feats = lax.dynamic_slice(own_bins, (reach, model_index * out_cols), (bins, out_cols))
        blocks = own_bins.reshape(own_bins.shape[0], windows, row_count).transpose(1, 0, 2)
        arrived = lax.all_to_all(blocks, "win", 0, 0, tiled=True)
        qkv_pieces = first_stage(qkv_own, 1)
        attention_pieces = qkv_pieces + first_stage(out_own, 1)
        partial = jnp.stack([conv_of(BF16, arrived[w]) for w in range(windows)])
        conv_pre = lax.all_to_all(partial, "win", 0, 0, tiled=True).astype(F32).sum(axis=0)

    conv_out = (own_feats + jax.nn.gelu(conv_pre + conv_bias)).astype(BF16)
    head_pieces = first_stage(head_own, 0, qkv_pieces[1:], conv_out)
    if stepwise:
        head_pieces.insert(2, across(head_pieces, ()))
    all_chan = lax.all_gather(conv_out, plane, axis=0)
    lists, _ = lax.optimization_barrier((exon_lists[:, 0], conv_out))
    counts = gene_counts(lists, bin_count)

    half = jax.ShapeDtypeStruct((segments * models // 2, bins, out_cols), BF16)
    keep, give = call_kernel(
        functools.partial(attention_kernel, segments),
        [half, half],
        place,
        win_ref,
        all_chan,
        *attention_pieces,
    )
    one = jax.ShapeDtypeStruct((bins, out_cols), BF16)
    own_sum, *sent_sums = call_kernel(
        pair_kernel,
        [jax.ShapeDtypeStruct(one.shape, F32), one, one, one],
        place,
        keep,
        swapped(give),
    )
    summed = own_sum
    for hop, x in enumerate(sent_sums, 1):
        pairs = [
            (s * models + m, (s ^ hop % 2) * models + (m ^ hop // 2 * 2))
            for s in range(segments)
            for m in range(models)
        ]
        summed = summed + lax.ppermute(x, plane, pairs).astype(F32)
    resid = (conv_out.astype(F32) + summed).astype(BF16)
    all_resid = plane_blocks(resid)

    sums_shape = jax.ShapeDtypeStruct((counts.shape[0], track_cols), BF16)
    if stepwise:
        own, below, far, above = head_pieces
        logits, far_rows = call_kernel(
            functools.partial(near_head_kernel, segments),
            [
                jax.ShapeDtypeStruct((bin_count, track_cols), F32),
                jax.ShapeDtypeStruct((bin_count, row_count), BF16),
            ],
            place,
            win_ref,
            *all_resid,
            own,
            below,
            above,
            scratch=all_blocks,
        )
        sums = call_kernel(
            far_head_kernel, sums_shape, logits, far_rows, far, bias_part[None, :], counts
        )
    else:
        sums = call_kernel(
            functools.partial(head_kernel, segments),
            sums_shape,
            place,
            win_ref,
            bias_part[None, :],
            counts,
            *all_resid,
            *head_pieces,
            scratch=all_blocks,
        )
    owners = segments * windows
    got = lax.all_to_all(
        sums.reshape(owners, GENE_DEV, track_cols), ("segment", "win"), 0, 0, tiled=True
    )
    got = got.astype(F32).reshape(segments, windows, GENE_DEV, track_cols).sum(axis=1)
    return jnp.log1p(got.transpose(1, 0, 2).reshape(GENE_DEV, segments * track_cols))


def solution(mesh):
    in_specs = (
        P("win", None, None),
        P("win", None, "mp"),
        P("mp"),
        P("win", "mp"),
        P("win", "mp"),
        P("win", "mp"),
        P("mp"),
        P(None, "win", None, None),
    )
    out_specs = P(("segment", "win"), "mp")
    return jax.shard_map(local, mesh=mesh, in_specs=in_specs, out_specs=out_specs, check_vma=False)
```
